32 devices in a mesh: head: 8 (over z, y), tok: 4 (over x, core).
Axes of the slice: x: 2, y: 2, z: 4, core: 2. Of those that a mesh axis runs over, the one named last changes fastest.
Arguments:
- queries: bfloat16 [512, 8192], P('tok', 'head'), may hold values from -6 to 6
- cache: bfloat16 [4, 2048, 256], P(None, 'tok'), may hold values from -6 to 6
- new_kv: bfloat16 [4, 512, 256], P(None, 'tok'), may hold values from -6 to 6
- q_gain: float32 [128], replicated, may hold values from 0.5 to 2.2
- k_gain: float32 [128], replicated, may hold values from 0.5 to 2.2
- out_weight: bfloat16 [8192, 4096], P('head'), may hold values from -0.5 to 0.5
- residual: bfloat16 [512, 4096], P(('tok', 'head')), may hold values from -3 to 3
- norm_gain: float32 [4096], replicated, may hold values from 0.25 to 1.75
- expert_ids: int32 [512, 8], P(('tok', 'head')), may hold values from 0 to 31, all different within a row; in each aligned block of 16 rows (0 to 15, 16 to 31, ...) at most 8 rows name the same one
- combine_weight: bfloat16 [512, 8], P(('tok', 'head')), may hold values from 0.049804688 to 0.5
- prefix_len: int32 [1], replicated, may hold values from 1024 to 2048
- w_gate_up: bfloat16 [32, 4096, 1536], P(('head', 'tok')), may hold values from -0.09375 to 0.09375
- w_down: bfloat16 [32, 768, 4096], P(('head', 'tok')), may hold values from -0.21875 to 0.21875
Outputs:
- layer_out: bfloat16 [512, 4096], P(('tok', 'head'))
The draws below stay inside these ranges and needn't reach their ends.
Inputs may be any that keep to these rules, and one draw needn't show every extreme that they name: `expert_ids`: in each aligned block of 16 rows (the rows of one device) no expert is named by more than 8 rows, and some expert reaches 8.
All inputs are finite; a program needn't handle non-finite values.
Results may differ from the reference program's by a relative error of at most 0.022.
Values may be sent and summed in bfloat16 or wider, within the bound.
A program may use at most 128 MiB of HBM per device.

```python
import math
import jax
import jax.numpy as jnp
import numpy as np
from jax import lax

D = 4096
HEADS = 64
KV_HEADS = 4
HD = 128
FFE = 768
TOPK = 8
ROWS_DEV = 16
TOKENS = 512
PREFIX = 2048
EXPERTS = 32
CAP = 8


def steps_of(key, dims, split, smallest, high):
    level, own = 1.0, jax.random.fold_in(key, 6)
    for dim, blocks in split:
        heights = jnp.exp(jax.random.uniform(jax.random.fold_in(own, dim), (blocks,), jnp.float32, smallest / len(split), high / len(split)))
        level = level * jnp.repeat(heights, dims[dim] // blocks).reshape([-1 if axis == dim else 1 for axis in range(len(dims))])
    return level


def routed_block(key, own, number, rows, amount, top, most, skew):
    ranking = jax.random.permutation(key, amount)
    packed, common = shares(amount, rows * top, most, skew, True), shares(amount, rows * top, most, skew, False)
    places = jnp.arange(amount)

    def named(sizes, turn):
        used = int((sizes > 0).sum())
        fixed = max(1, used // 4)
        moved = fixed + (places - fixed + turn * (used - fixed)) % max(1, amount - fixed)
        return jnp.zeros((amount,), jnp.int32).at[ranking[jnp.where(places < fixed, places, moved)]].set(jnp.asarray(sizes, jnp.int32))

    sizes = jnp.where(number % 4 == 0, named(packed, number // 4), named(common, number - number // 4 - 1))
    mixed = jax.random.permutation(jax.random.fold_in(own, 3), amount)
    giver, sink = mixed[0:amount // 2 * 2:2], mixed[1:amount // 2 * 2:2]
    slack = jnp.minimum(sizes[giver] - 1, most - sizes[sink]) // 2
    slack = jnp.where((giver == ranking[0]) | (sink == ranking[0]) | (sizes[sink] == 0), 0, jnp.maximum(slack, 0))
    moved = jax.random.randint(jax.random.fold_in(own, 4), (amount // 2,), 0, 1 << 20) % (slack + 1)
    sizes = sizes.at[giver].add(-moved).at[sink].add(moved)
    items = jnp.searchsorted(jnp.cumsum(sizes), jnp.arange(rows * top), side="right").astype(jnp.int32)
    grid = items.reshape(top, rows).T
    grid = grid[jax.random.permutation(jax.random.fold_in(own, 1), rows)]
    turn = jax.random.randint(jax.random.fold_in(own, 2), (rows, 1), 0, top)
    return jnp.take_along_axis(grid, (jnp.arange(top)[None, :] + turn) % top, axis=1)


def shares(amount, total, bound, skew, full):
    weights = [(1 << 20) // math.isqrt(rank ** skew) + 1 for rank in range(1, amount + 1)]
    largest = bound if full else min(bound, max(-(-total // amount), total * weights[0] // sum(weights)))
    least = 1 if total - largest >= amount - 1 else 0
    holding, rest = [largest] + [least] * (amount - 1), total - largest - least * (amount - 1)
    while rest > 0:
        candidates = [i for i in range(1, amount) if holding[i] < largest] or [i for i in range(1, amount) if holding[i] < bound]
        pool, remaining = sum([weights[i] for i in candidates]), rest
        for i in candidates:
            extra = min(bound - holding[i], max(1, remaining * weights[i] // pool), rest)
            holding[i] = holding[i] + extra
            rest = rest - extra
    return np.array(holding)


def normal_values(key, extent, spread, bound, split=(), held_as=jnp.bfloat16):
    drawn = spread * jax.random.normal(key, extent, jnp.float32)
    if split:
        drawn = drawn * steps_of(key, extent, split, -0.22, 0.18)
    return jnp.clip(drawn, -bound, bound).astype(held_as)


def setup_inputs(seed: int = 0) -> dict:
    key_list = jax.random.split(jax.random.key(seed), 14)
    queries = normal_values(key_list[0], (TOKENS, HEADS * HD), 1.0, 6.0, ((0, 4), (1, 8)))
    cache = normal_values(key_list[1], (KV_HEADS, PREFIX, 2 * HD), 1.0, 6.0, ((1, 4),))
    new_kv = normal_values(key_list[2], (KV_HEADS, TOKENS, 2 * HD), 1.0, 6.0, ((1, 4),))
    q_gain = jnp.clip(jnp.exp(jax.random.uniform(key_list[3], (HD,), jnp.float32, math.log(0.5), math.log(2.2))), 0.5, 2.2)
    k_gain = jnp.clip(jnp.exp(jax.random.uniform(key_list[4], (HD,), jnp.float32, math.log(0.5), math.log(2.2))), 0.5, 2.2)
    out_weight = normal_values(key_list[5], (HEADS * HD, D), HD ** -0.5, 0.5, ((0, 8),))
    residual = normal_values(key_list[6], (TOKENS, D), 0.5, 3.0, ((0, 32),))
    norm_gain = jnp.clip(1.0 + 0.15 * jax.random.normal(key_list[7], (D,), jnp.float32), 0.25, 1.75)
    expert_ids_keys = jax.random.split(jax.random.fold_in(key_list[8], 1), TOKENS // ROWS_DEV)
    expert_ids_turns = jax.random.permutation(jax.random.fold_in(key_list[8], 3), TOKENS // ROWS_DEV)
    expert_ids = jax.vmap(lambda own, number: routed_block(jax.random.fold_in(key_list[8], 2), own, number, ROWS_DEV, EXPERTS, TOPK, CAP, 2))(expert_ids_keys, expert_ids_turns).reshape((TOKENS, TOPK))
    combine_weight = jnp.clip(jnp.exp(math.log(0.5) - 2.306499 * jax.random.uniform(key_list[9], (TOKENS, TOPK), jnp.float32) ** steps_of(key_list[9], (TOKENS, TOPK), ((0, 32),), -0.2, 0.2)), 0.049804688, 0.5).astype(jnp.bfloat16)
    prefix_len = jax.random.randint(key_list[10], (1,), PREFIX // 2, PREFIX + 1).astype(jnp.int32)
    w_gate_up = normal_values(key_list[11], (EXPERTS, D, 2 * FFE), D ** -0.5, 0.09375, ((0, 32),))
    w_down = normal_values(key_list[12], (EXPERTS, FFE, D), FFE ** -0.5, 0.21875, ((0, 32),))
    return {"queries": queries, "cache": cache, "new_kv": new_kv, "q_gain": q_gain, "k_gain": k_gain, "out_weight": out_weight, "residual": residual, "norm_gain": norm_gain, "expert_ids": expert_ids, "combine_weight": combine_weight, "prefix_len": prefix_len, "w_gate_up": w_gate_up, "w_down": w_down}


EPSILON = 1e-06

def rms_scale(values, gain):
    mean_square = lax.optimization_barrier(jnp.mean(values * values, axis=-1, keepdims=True))
    return values * lax.rsqrt(mean_square + EPSILON) * gain

def normed_block(block, k_gain):
    key_part = rms_scale(block[:, :HD].astype(jnp.float32), k_gain).astype(jnp.bfloat16)
    return jnp.concatenate([key_part, block[:, HD:]], axis=1)

def reference(queries, cache, new_kv, q_gain, k_gain, out_weight, residual, norm_gain, expert_ids, combine_weight, prefix_len, w_gate_up, w_down):
    group_size = HEADS // KV_HEADS
    query_all = rms_scale(queries.reshape(TOKENS, HEADS, HD).astype(jnp.float32), q_gain).astype(jnp.bfloat16)
    key_position = jnp.arange(PREFIX + TOKENS, dtype=jnp.int32)
    query_position = jnp.arange(TOKENS, dtype=jnp.int32)
    visible = jnp.where(key_position[None, :] < PREFIX, key_position[None, :] < prefix_len[0], key_position[None, :] - PREFIX <= query_position[:, None])

    def one_head(head_index):
        kv_head = head_index // group_size
        keyval = jnp.concatenate([lax.dynamic_index_in_dim(cache, kv_head, 0, keepdims=False), lax.dynamic_index_in_dim(new_kv, kv_head, 0, keepdims=False)], axis=0)
        keyval = normed_block(keyval, k_gain)
        query_head = lax.dynamic_index_in_dim(query_all, head_index, 1, keepdims=False)
        scores = jnp.dot(query_head, keyval[:, :HD].T, preferred_element_type=jnp.float32) * HD ** (-0.5)
        weights = jnp.where(visible, jnp.exp(scores), 0.0)
        total = lax.optimization_barrier(jnp.sum(weights, axis=1, keepdims=True))
        mixed = jnp.dot(weights.astype(jnp.bfloat16), keyval[:, HD:], preferred_element_type=jnp.float32)
        return (mixed / total).astype(jnp.bfloat16)
    per_head = lax.map(one_head, jnp.arange(HEADS, dtype=jnp.int32))
    attn = jnp.transpose(per_head, (1, 0, 2)).reshape(TOKENS, HEADS * HD)
    hidden = residual.astype(jnp.float32) + jnp.dot(attn, out_weight, preferred_element_type=jnp.float32)
    normed = rms_scale(hidden, norm_gain.astype(jnp.float32)).astype(jnp.bfloat16)
    blocks = TOKENS // ROWS_DEV
    flat_ids = expert_ids.reshape(blocks, ROWS_DEV * TOPK).astype(jnp.int32)
    onehot = (flat_ids[:, :, None] == jnp.arange(EXPERTS, dtype=jnp.int32)[None, None, :]).astype(jnp.int32)
    before = jnp.cumsum(onehot, axis=1) - onehot
    slot_index = lax.optimization_barrier(jnp.sum(before * onehot, axis=2)).astype(jnp.int32)
    token_index = jnp.repeat(jnp.arange(TOKENS, dtype=jnp.int32).reshape(blocks, ROWS_DEV), TOPK, axis=1)
    block_index = jnp.broadcast_to(jnp.arange(blocks, dtype=jnp.int32)[:, None], flat_ids.shape)
    table = jnp.full((EXPERTS, blocks, CAP), TOKENS, jnp.int32).at[flat_ids, block_index, slot_index].set(token_index)
    padded = jnp.concatenate([normed, jnp.zeros((1, D), jnp.bfloat16)], axis=0)

    def one_expert(expert_index):
        picked_rows = padded[table[expert_index].reshape(-1)]
        both = jnp.dot(picked_rows, w_gate_up[expert_index], preferred_element_type=jnp.float32)
        active = (jax.nn.silu(both[:, :FFE]) * both[:, FFE:]).astype(jnp.bfloat16)
        return jnp.dot(active, w_down[expert_index], preferred_element_type=jnp.float32).astype(jnp.bfloat16)
    outputs = lax.map(one_expert, jnp.arange(EXPERTS, dtype=jnp.int32))
    position = (block_index * CAP + slot_index).reshape(TOKENS, TOPK)
    gathered = outputs[flat_ids.reshape(TOKENS, TOPK), position]
    expert_sum = jnp.einsum('tk,tkd->td', combine_weight.astype(jnp.float32), gathered.astype(jnp.float32))
    return (hidden + expert_sum).astype(jnp.bfloat16)
```

```python
import functools

import jax
import jax.numpy as jnp
from jax import lax
from jax.experimental import pallas as pl
from jax.experimental.pallas import tpu as pltpu
from jax.sharding import PartitionSpec as P

HEADS = 64
KV_HEADS = 4
HD = 128


EPSILON = 1e-06


def rms_scale(values, gain):
    mean_square = jnp.mean(values * values, axis=-1, keepdims=True)
    return values * lax.rsqrt(mean_square + EPSILON) * gain


def expert_block(inputs, gate_up, down_proj):
    width = down_proj.shape[1]
    hidden_units = down_proj.shape[0]
    flat_rows = inputs.reshape(-1, width)
    both = jnp.dot(flat_rows, gate_up, preferred_element_type=jnp.float32)
    active = (jax.nn.silu(both[:, :hidden_units]) * both[:, hidden_units:]).astype(jnp.bfloat16)
    result = jnp.dot(active, down_proj, preferred_element_type=jnp.float32).astype(jnp.bfloat16)
    return result.reshape(inputs.shape)


DEPTH = 4
CORES = 2
CHUNKS = 4
VMEM_BYTES = 60 * 2**20
MESH = pl.DeviceIdType.MESH


def dot32(a, b):
    return jnp.dot(a, b, preferred_element_type=jnp.float32)


def layer_kernel(
    dims,
    attn_ref,
    out_weight_hbm,
    residual_ref,
    gain_ref,
    place_row_ref,
    place_col_ref,
    scale_col_ref,
    gate_up_hbm,
    down_hbm,
    result_ref,
    out_w,
    gate_up,
    down,
    part,
    part_y,
    sum_y,
    part_z,
    hidden,
    rows,
    acc,
    active,
    share,
    in_core,
    sum_core,
    in_ax,
    in_ay,
    sum_ax,
    sum_ay,
    in_bx,
    in_by,
    sum_b,
    in_z,
    load_sem,
    send_sem,
    recv_sem,
):
    nz, ny, nx, slots = dims
    head, tok = lax.axis_index("head"), lax.axis_index("tok")
    z, y = lax.div(head, ny), lax.rem(head, ny)
    x, core = lax.div(tok, CORES), lax.rem(tok, CORES)
    width = hidden.shape[1]
    step = width // CHUNKS
    tokens = place_row_ref.shape[1]
    hidden_units = down.shape[0]
    columns = [pl.ds(k * step, step) for k in range(CHUNKS)]

    axes = {
        "z": (nz, z, lambda p: (p * ny + y, tok)),
        "y": (ny, y, lambda p: (z * ny + p, tok)),
        "x": (nx, x, lambda p: (head, p * CORES + core)),
        "core": (CORES, core, lambda p: (head, x * CORES + p)),
    }

    loads = []

    def load(src, dst):
        copy = pltpu.make_async_copy(src, dst, load_sem.at[len(loads)])
        copy.start()
        loads.append(copy)
        return copy

    out_w_loads = [load(out_weight_hbm.at[:, c], out_w.at[:, c]) for c in columns]
    gate_up_loads = [load(gate_up_hbm.at[0, c, :], gate_up.at[c, :]) for c in columns]
    down_loads = [load(down_hbm.at[0, :, c], down.at[:, c]) for c in columns]

    barrier = pltpu.get_barrier_semaphore()
    greeted = 0
    for n, me, device in axes.values():
        for i in range(1, n):
            pl.semaphore_signal(
                barrier, inc=1, device_id=device(lax.rem(me + i, n)), device_id_type=MESH
            )
            greeted += 1
    pl.semaphore_wait(barrier, greeted)

    sends = []

    def send(stage, k, axis, source, target):
        n, me, device = axes[axis]
        for i in range(1, n):
            peer = lax.rem(me + i, n)
            copy = pltpu.make_async_remote_copy(
                src_ref=source(peer),
                dst_ref=target(i),
                send_sem=send_sem.at[stage, k, i - 1],
                recv_sem=recv_sem.at[stage, k, i - 1],
                device_id=device(peer),
                device_id_type=MESH,
            )
            copy.start()
            sends.append(copy)

    def arrive(stage, k, axis, region):
        n, me, device = axes[axis]
        for i in range(1, n):
            peer = lax.rem(me + n - i, n)
            place = region(i, peer)
            pltpu.make_async_remote_copy(
                src_ref=place,
                dst_ref=place,
                send_sem=send_sem.at[stage, k, i - 1],
                recv_sem=recv_sem.at[stage, k, i - 1],
                device_id=device(peer),
                device_id_type=MESH,
            ).wait_recv()

    def total(first, others):
        value = first.astype(jnp.float32)
        for other in others:
            value = value + other.astype(jnp.float32)
        return value

    for k, c in enumerate(columns):
        out_w_loads[k].wait()
        proj = dot32(attn_ref[...], out_w[:, c]).astype(jnp.bfloat16)
        part[:, :, :, c] = proj.reshape(nz, ny, -1, step)
        send(0, k, "y", lambda p: part.at[:, p, :, c], lambda i: part_y.at[i - 1, :, :, c])
    for k, c in enumerate(columns):
        arrive(0, k, "y", lambda i, p: part_y.at[i - 1, :, :, c])
        value = total(part[:, y, :, c], [part_y[i, :, :, c] for i in range(ny - 1)])
        sum_y[:, :, c] = value.astype(jnp.bfloat16)
        send(1, k, "z", lambda p: sum_y.at[p, :, c], lambda i: part_z.at[i - 1, :, c])
    square = jnp.zeros((hidden.shape[0], 1), jnp.float32)
    for k, c in enumerate(columns):
        arrive(1, k, "z", lambda i, p: part_z.at[i - 1, :, c])
        value = total(sum_y[z, :, c], [part_z[i, :, c] for i in range(nz - 1)])
        value = value + residual_ref[:, c].astype(jnp.float32)
        hidden[:, c] = value
        square = square + jnp.sum(value * value, axis=1, keepdims=True)
    scale = lax.rsqrt(square / width + EPSILON)

    for k, c in enumerate(columns):
        rows[tok, z, y, :, c] = (hidden[:, c] * scale * gain_ref[:, c]).astype(jnp.bfloat16)
        mine = lambda _: rows.at[tok, z, y, :, c]
        send(2, k, "z", mine, mine)
    for k, c in enumerate(columns):
        arrive(2, k, "z", lambda i, p: rows.at[tok, p, y, :, c])
        mine = lambda _: rows.at[tok, :, y, :, c]
        send(3, k, "xy"[k % 2], mine, mine)
    for k, c in enumerate(columns):
        if k % 2 == 0:
            arrive(3, k, "x", lambda i, p: rows.at[p * CORES + core, :, y, :, c])
            for q in range(nx):
                mine = lambda _: rows.at[q * CORES + core, :, y, :, c]
                send(4 + q, k, "y", mine, mine)
        else:
            arrive(3, k, "y", lambda i, p: rows.at[tok, :, p, :, c])
            mine = lambda _: rows.at[tok, :, :, :, c]
            send(4, k, "x", mine, mine)
    base = 4 + nx
    for k, c in enumerate(columns):
        if k % 2 == 0:
            for q in range(nx):
                arrive(4 + q, k, "y", lambda i, p: rows.at[q * CORES + core, :, p, :, c])
        else:
            arrive(4, k, "x", lambda i, p: rows.at[p * CORES + core, :, :, :, c])
        for q in range(nx):
            mine = lambda _: rows.at[q * CORES + core, :, :, :, c]
            send(base + q, k, "core", mine, mine)
    select = (
        lax.broadcasted_iota(jnp.int32, (slots, tokens), 0) == place_row_ref[...]
    ).astype(jnp.bfloat16)
    for k, c in enumerate(columns):
        for q in range(nx):
            arrive(base + q, k, "core", lambda i, p: rows.at[q * CORES + p, :, :, :, c])
        picked = dot32(select, rows[:, :, :, :, c].reshape(tokens, step)).astype(jnp.bfloat16)
        gate_up_loads[k].wait()
        both = dot32(picked, gate_up[c, :])
        acc[...] = both if k == 0 else acc[...] + both
    base += nx

    gate = acc[:, :hidden_units]
    active[...] = (jax.nn.silu(gate) * acc[:, hidden_units:]).astype(jnp.bfloat16)
    spread = jnp.where(
        lax.broadcasted_iota(jnp.int32, (tokens, slots), 1) == place_col_ref[...],
        scale_col_ref[...],
        0.0,
    ).astype(jnp.bfloat16)

    for k, c in enumerate(columns):
        down_loads[k].wait()
        expert_out = dot32(active[...], down[:, c]).astype(jnp.bfloat16)
        weighted = dot32(spread, expert_out).astype(jnp.bfloat16)
        share[:, :, :, :, :, c] = weighted.reshape(nx, CORES, nz, ny, -1, step)
        send(
            base, k, "core",
            lambda p: share.at[:, p, :, :, :, c],
            lambda i: in_core.at[:, :, :, :, c],
        )
    for k, c in enumerate(columns):
        arrive(base, k, "core", lambda i, p: in_core.at[:, :, :, :, c])
        value = total(share[:, core, :, :, :, c], [in_core[:, :, :, :, c]])
        sum_core[:, :, :, :, c] = value.astype(jnp.bfloat16)
        if k % 2 == 0:
            send(
                base + 1, k, "x",
                lambda p: sum_core.at[p, :, :, :, c],
                lambda i: in_ax.at[i - 1, :, :, :, c],
            )
        else:
            send(
                base + 1, k, "y",
                lambda p: sum_core.at[:, :, p, :, c],
                lambda i: in_ay.at[i - 1, :, :, :, c],
            )
    for k, c in enumerate(columns):
        if k % 2 == 0:
            arrive(base + 1, k, "x", lambda i, p: in_ax.at[i - 1, :, :, :, c])
            value = total(
                sum_core[x, :, :, :, c], [in_ax[i, :, :, :, c] for i in range(nx - 1)]
            )
            sum_ax[:, :, :, c] = value.astype(jnp.bfloat16)
            send(
                base + 2, k, "y",
                lambda p: sum_ax.at[:, p, :, c],
                lambda i: in_by.at[i - 1, :, :, c],
            )
        else:
            arrive(base + 1, k, "y", lambda i, p: in_ay.at[i - 1, :, :, :, c])
            value = total(
                sum_core[:, :, y, :, c], [in_ay[i, :, :, :, c] for i in range(ny - 1)]
            )
            sum_ay[:, :, :, c] = value.astype(jnp.bfloat16)
            send(
                base + 2, k, "x",
                lambda p: sum_ay.at[p, :, :, c],
                lambda i: in_bx.at[i - 1, :, :, c],
            )
    for k, c in enumerate(columns):
        if k % 2 == 0:
            arrive(base + 2, k, "y", lambda i, p: in_by.at[i - 1, :, :, c])
            value = total(sum_ax[:, y, :, c], [in_by[i, :, :, c] for i in range(ny - 1)])
        else:
            arrive(base + 2, k, "x", lambda i, p: in_bx.at[i - 1, :, :, c])
            value = total(sum_ay[x, :, :, c], [in_bx[i, :, :, c] for i in range(nx - 1)])
        sum_b[:, :, c] = value.astype(jnp.bfloat16)
        send(base + 3, k, "z", lambda p: sum_b.at[p, :, c], lambda i: in_z.at[i - 1, :, c])
    for k, c in enumerate(columns):
        arrive(base + 3, k, "z", lambda i, p: in_z.at[i - 1, :, c])
        value = total(sum_b[z, :, c], [in_z[i, :, c] for i in range(nz - 1)])
        result_ref[:, c] = (hidden[:, c] + value).astype(jnp.bfloat16)
    for copy in sends:
        copy.wait_send()


def routed_layer(
    attn, out_weight, residual, norm_gain, expert_ids, combine_weight, w_gate_up, w_down
):
    head_count = lax.axis_size("head")
    tok_count = lax.axis_size("tok")
    nz, ny, nx = DEPTH, head_count // DEPTH, tok_count // CORES
    width = out_weight.shape[1]
    rows_out, topk = expert_ids.shape
    experts_all = head_count * tok_count
    tokens = rows_out * experts_all
    capacity = max(2, 2 * rows_out * topk // experts_all)
    slots = experts_all * capacity
    hidden_units = w_down.shape[1]

    routing = lax.all_gather(
        jnp.concatenate([expert_ids.astype(jnp.bfloat16), combine_weight], axis=1),
        ("tok", "head"),
        axis=0,
        tiled=True,
    )
    own = lax.axis_index("head") * tok_count + lax.axis_index("tok")
    named = routing[:, :topk].astype(jnp.int32) == own
    chosen = jnp.any(named, axis=1)
    scale = jnp.sum(jnp.where(named, routing[:, topk:].astype(jnp.float32), 0.0), axis=1)
    blocks = chosen.reshape(experts_all, rows_out).astype(jnp.int32)
    earlier = jnp.arange(rows_out)[:, None] < jnp.arange(rows_out)[None, :]
    before = jnp.sum(jnp.where(earlier[None], blocks[:, :, None], 0), axis=1)
    place = jnp.arange(experts_all, dtype=jnp.int32)[:, None] * capacity + before
    place = jnp.where(chosen, place.reshape(-1), -1)

    b16, f32 = jnp.bfloat16, jnp.float32
    vmem = pl.BlockSpec(memory_space=pltpu.VMEM)
    hbm = pl.BlockSpec(memory_space=pl.ANY)
    stages = 8 + 2 * nx
    widest = max(nz, ny, nx, CORES) - 1
    scratch = [
        pltpu.VMEM(out_weight.shape, b16),
        pltpu.VMEM(w_gate_up.shape[1:], b16),
        pltpu.VMEM(w_down.shape[1:], b16),
        pltpu.VMEM((nz, ny, rows_out, width), b16),
        pltpu.VMEM((ny - 1, nz, rows_out, width), b16),
        pltpu.VMEM((nz, rows_out, width), b16),
        pltpu.VMEM((nz - 1, rows_out, width), b16),
        pltpu.VMEM((rows_out, width), f32),
        pltpu.VMEM((tok_count, nz, ny, rows_out, width), b16),
        pltpu.VMEM((slots, 2 * hidden_units), f32),
        pltpu.VMEM((slots, hidden_units), b16),
        pltpu.VMEM((nx, CORES, nz, ny, rows_out, width), b16),
        pltpu.VMEM((nx, nz, ny, rows_out, width), b16),
        pltpu.VMEM((nx, nz, ny, rows_out, width), b16),
        pltpu.VMEM((nx - 1, nz, ny, rows_out, width), b16),
        pltpu.VMEM((ny - 1, nx, nz, rows_out, width), b16),
        pltpu.VMEM((nz, ny, rows_out, width), b16),
        pltpu.VMEM((nx, nz, rows_out, width), b16),
        pltpu.VMEM((nx - 1, nz, rows_out, width), b16),
        pltpu.VMEM((ny - 1, nz, rows_out, width), b16),
        pltpu.VMEM((nz, rows_out, width), b16),
        pltpu.VMEM((nz - 1, rows_out, width), b16),
        pltpu.SemaphoreType.DMA((3 * CHUNKS,)),
        pltpu.SemaphoreType.DMA((stages, CHUNKS, widest)),
        pltpu.SemaphoreType.DMA((stages, CHUNKS, widest)),
    ]
    return pl.pallas_call(
        functools.partial(layer_kernel, (nz, ny, nx, slots)),
        out_shape=jax.ShapeDtypeStruct((rows_out, width), b16),
        in_specs=[vmem, hbm, vmem, vmem, vmem, vmem, vmem, hbm, hbm],
        out_specs=vmem,
        scratch_shapes=scratch,
        compiler_params=pltpu.CompilerParams(
            collective_id=0, has_side_effects=True, vmem_limit_bytes=VMEM_BYTES
        ),
    )(
        attn,
        out_weight,
        residual,
        norm_gain.reshape(1, width),
        place.reshape(1, tokens),
        place.reshape(tokens, 1),
        scale.reshape(tokens, 1),
        w_gate_up,
        w_down,
    )


def fits(tokens, width, experts):
    return 12 * tokens * width <= VMEM_BYTES // 2 and experts <= 256


def per_device(
    queries,
    cache,
    new_kv,
    q_gain,
    k_gain,
    out_weight,
    residual,
    norm_gain,
    expert_ids,
    combine_weight,
    prefix_len,
    w_gate_up,
    w_down,
):
    head_count = lax.axis_size("head")
    tok_count = lax.axis_size("tok")
    query_rows = queries.shape[0]
    local_heads = queries.shape[1] // HD
    cache_rows = cache.shape[1]
    segment = cache_rows + query_rows
    kv_index = lax.axis_index("head") * local_heads // (HEADS // KV_HEADS)
    query_normed = rms_scale(
        queries.reshape(query_rows, local_heads, HD).astype(jnp.float32), q_gain
    ).astype(jnp.bfloat16)
    own_block = jnp.concatenate(
        [
            lax.dynamic_index_in_dim(cache, kv_index, 0, keepdims=False),
            lax.dynamic_index_in_dim(new_kv, kv_index, 0, keepdims=False),
        ],
        axis=0,
    )
    key_part = rms_scale(own_block[:, :HD].astype(jnp.float32), k_gain).astype(jnp.bfloat16)
    key_block = jnp.concatenate([key_part, own_block[:, HD:]], axis=1)
    query_position = lax.axis_index("tok") * query_rows + jnp.arange(query_rows, dtype=jnp.int32)
    limit = prefix_len[0]
    piece = lax.all_gather(key_block, "tok", axis=0, tiled=True)
    position = jnp.arange(piece.shape[0], dtype=jnp.int32)
    shard = position // segment
    offset = position % segment
    in_cache = offset < cache_rows
    cache_position = shard * cache_rows + offset
    span_position = shard * query_rows + offset - cache_rows
    visible = jnp.where(
        in_cache[None, :],
        (cache_position < limit)[None, :],
        span_position[None, :] <= query_position[:, None],
    )
    scores = jnp.einsum(
        "qhd,kd->qhk", query_normed, piece[:, :HD], preferred_element_type=jnp.float32
    ) * HD ** (-0.5)
    weights = jnp.where(visible[:, None, :], jnp.exp(scores), 0.0)
    accum = jnp.einsum(
        "qhk,kd->qhd",
        weights.astype(jnp.bfloat16),
        piece[:, HD:],
        preferred_element_type=jnp.float32,
    )
    total = jnp.sum(weights, axis=2)
    accum, total = (accum, total)
    attn = (accum / total[:, :, None]).astype(jnp.bfloat16).reshape(query_rows, local_heads * HD)
    experts_total = head_count * tok_count
    if fits(query_rows * tok_count, out_weight.shape[1], experts_total):
        return routed_layer(
            attn, out_weight, residual, norm_gain, expert_ids, combine_weight, w_gate_up, w_down
        )
    rows_out = query_rows // head_count
    full_proj = lax.psum(
        jnp.dot(attn, out_weight, preferred_element_type=jnp.float32).astype(jnp.bfloat16), "head"
    ).astype(jnp.float32)
    attn_proj = lax.dynamic_slice_in_dim(full_proj, lax.axis_index("head") * rows_out, rows_out, 0)
    hidden = residual.astype(jnp.float32) + attn_proj
    normed = rms_scale(hidden, norm_gain).astype(jnp.bfloat16)
    width = normed.shape[1]
    experts_all = head_count * tok_count
    topk = expert_ids.shape[1]
    capacity = max(2, 2 * rows_out * topk // experts_all)
    flat_ids = expert_ids.reshape(-1)
    onehot = (flat_ids[:, None] == jnp.arange(experts_all, dtype=jnp.int32)[None, :]).astype(
        jnp.int32
    )
    before = jnp.cumsum(onehot, axis=0) - onehot
    slot_index = jnp.sum(before * onehot, axis=1)
    target = (flat_ids * capacity + slot_index).reshape(rows_out, topk)
    matches = (
        target[:, :, None] == jnp.arange(experts_all * capacity, dtype=jnp.int32)[None, None, :]
    )
    placing = jnp.sum(matches.astype(jnp.int32), axis=1).astype(jnp.bfloat16)
    mixing = jnp.sum(
        jnp.where(matches, combine_weight.astype(jnp.float32)[:, :, None], 0.0), axis=1
    ).astype(jnp.bfloat16)
    outgoing = jnp.einsum("rs,rd->sd", placing, normed, preferred_element_type=jnp.float32).astype(
        jnp.bfloat16
    )
    outgoing = outgoing.reshape(experts_all, capacity, width)
    returned = lax.all_to_all(
        expert_block(
            lax.all_to_all(outgoing, ("head", "tok"), split_axis=0, concat_axis=0, tiled=True),
            w_gate_up[0],
            w_down[0],
        ),
        ("head", "tok"),
        split_axis=0,
        concat_axis=0,
        tiled=True,
    )
    back_rows = returned.reshape(experts_all * capacity, width)
    expert_sum = jnp.dot(mixing, back_rows, preferred_element_type=jnp.float32)
    return (hidden + expert_sum).astype(jnp.bfloat16)

def solution(mesh):
    placed = (
        P("tok", "head"),
        P(None, "tok", None),
        P(None, "tok", None),
        P(),
        P(),
        P("head", None),
        P(("tok", "head"), None),
        P(),
        P(("tok", "head"), None),
        P(("tok", "head"), None),
        P(),
        P(("head", "tok"), None, None),
        P(("head", "tok"), None, None),
    )
    return jax.shard_map(
        per_device, mesh=mesh, in_specs=placed, out_specs=P(("tok", "head"), None), check_vma=False
    )
```

```python
import functools

import jax
import jax.numpy as jnp
from jax import lax
from jax.experimental import pallas as pl
from jax.experimental.pallas import tpu as pltpu
from jax.sharding import PartitionSpec as P

HEADS = 64
KV_HEADS = 4
HD = 128


EPSILON = 1e-06


def rms_scale(values, gain):
    mean_square = jnp.mean(values * values, axis=-1, keepdims=True)
    return values * lax.rsqrt(mean_square + EPSILON) * gain


def expert_block(inputs, gate_up, down_proj):
    width = down_proj.shape[1]
    hidden_units = down_proj.shape[0]
    flat_rows = inputs.reshape(-1, width)
    both = jnp.dot(flat_rows, gate_up, preferred_element_type=jnp.float32)
    active = (jax.nn.silu(both[:, :hidden_units]) * both[:, hidden_units:]).astype(jnp.bfloat16)
    result = jnp.dot(active, down_proj, preferred_element_type=jnp.float32).astype(jnp.bfloat16)
    return result.reshape(inputs.shape)


DEPTH = 4
CORES = 2
CHUNKS = 4
VMEM_BYTES = 60 * 2**20
MESH = pl.DeviceIdType.MESH


def dot32(a, b):
    return jnp.dot(a, b, preferred_element_type=jnp.float32)


def layer_kernel(
    dims,
    queries_hbm,
    cache_hbm,
    new_kv_hbm,
    q_gain_ref,
    k_gain_ref,
    limit_ref,
    out_weight_hbm,
    residual_ref,
    gain_ref,
    ids_ref,
    combine_ref,
    gate_up_hbm,
    down_hbm,
    result_ref,
    queries,
    keyval,
    query_normed,
    mixed,
    weight_sum,
    attn,
    routing,
    select,
    spread,
    out_w,
    gate_up,
    down,
    part,
    part_y,
    sum_y,
    part_z,
    hidden,
    rows,
    acc,
    active,
    share,
    in_core,
    sum_core,
    in_ax,
    in_ay,
    sum_ax,
    sum_ay,
    in_bx,
    in_by,
    sum_b,
    in_z,
    load_sem,
    send_sem,
    recv_sem,
):
    nz, ny, nx, capacity = dims
    head, tok = lax.axis_index("head"), lax.axis_index("tok")
    z, y = lax.div(head, ny), lax.rem(head, ny)
    x, core = lax.div(tok, CORES), lax.rem(tok, CORES)
    tok_count = nx * CORES
    width = hidden.shape[1]
    rows_out = hidden.shape[0]
    step = width // CHUNKS
    slots, tokens = select.shape
    topk = ids_ref.shape[1]
    hidden_units = down.shape[0]
    query_rows = queries.shape[0]
    local_heads = queries.shape[1] // HD
    cache_rows = cache_hbm.shape[1]
    segment = keyval.shape[1]
    columns = [pl.ds(k * step, step) for k in range(CHUNKS)]
    spans = columns[:-1] + [pl.ds(width - step, step + 128)]

    axes = {
        "z": (nz, z, lambda p: (p * ny + y, tok)),
        "y": (ny, y, lambda p: (z * ny + p, tok)),
        "x": (nx, x, lambda p: (head, p * CORES + core)),
        "core": (CORES, core, lambda p: (head, x * CORES + p)),
    }

    loads = []

    def load(src, dst):
        copy = pltpu.make_async_copy(src, dst, load_sem.at[len(loads)])
        copy.start()
        loads.append(copy)
        return copy

    kv_index = lax.div(head * local_heads, HEADS // KV_HEADS)
    kv_loads = [
        load(cache_hbm.at[kv_index], keyval.at[tok, pl.ds(0, cache_rows)]),
        load(new_kv_hbm.at[kv_index], keyval.at[tok, pl.ds(cache_rows, query_rows)]),
    ]
    query_load = load(queries_hbm, queries)
    out_w_loads = [load(out_weight_hbm.at[:, c], out_w.at[:, c]) for c in columns]
    gate_up_loads = [load(gate_up_hbm.at[0, c, :], gate_up.at[c, :]) for c in columns]
    down_loads = [load(down_hbm.at[0, :, c], down.at[:, c]) for c in columns]

    barrier = pltpu.get_barrier_semaphore()
    greeted = 0
    for n, me, device in axes.values():
        for i in range(1, n):
            pl.semaphore_signal(
                barrier, inc=1, device_id=device(lax.rem(me + i, n)), device_id_type=MESH
            )
            greeted += 1

    sends = []

    def send(stage, k, axis, source, target):
        n, me, device = axes[axis]
        for i in range(1, n):
            peer = lax.rem(me + i, n)
            copy = pltpu.make_async_remote_copy(
                src_ref=source(peer),
                dst_ref=target(i),
                send_sem=send_sem.at[stage, k, i - 1],
                recv_sem=recv_sem.at[stage, k, i - 1],
                device_id=device(peer),
                device_id_type=MESH,
            )
            copy.start()
            sends.append(copy)

    def spread_out(stage, k, axis, place):
        send(stage, k, axis, lambda _: place, lambda _: place)

    def arrive(stage, k, axis, region):
        n, me, device = axes[axis]
        for i in range(1, n):
            peer = lax.rem(me + n - i, n)
            place = region(i, peer)
            pltpu.make_async_remote_copy(
                src_ref=place,
                dst_ref=place,
                send_sem=send_sem.at[stage, k, i - 1],
                recv_sem=recv_sem.at[stage, k, i - 1],
                device_id=device(peer),
                device_id_type=MESH,
            ).wait_recv()

    def total(first, others):
        value = first.astype(jnp.float32)
        for other in others:
            value = value + other.astype(jnp.float32)
        return value

    def wavefront(stages):
        for turn in range(CHUNKS + len(stages) - 1):
            for place in reversed(range(len(stages))):
                if 0 <= turn - place < CHUNKS:
                    stages[place](turn - place)

    routing[tok, z, y, :, :] = jnp.full((rows_out, 256), -1.0, jnp.bfloat16)
    routing[tok, z, y, :, pl.ds(0, topk)] = (
        ids_ref[...].astype(jnp.float32).astype(jnp.bfloat16)
    )
    routing[tok, z, y, :, pl.ds(128, topk)] = combine_ref[...]
    for copy in kv_loads:
        copy.wait()
    keyval[tok, :, :HD] = rms_scale(
        keyval[tok, :, :HD].astype(jnp.float32), k_gain_ref[...]
    ).astype(jnp.bfloat16)
    pl.semaphore_wait(barrier, greeted)
    spread_out(0, 0, "x", keyval.at[tok])
    spread_out(1, 0, "core", keyval.at[tok])
    spread_out(2, 0, "z", routing.at[tok, z, y])
    query_load.wait()
    for j in range(local_heads):
        query_normed[j] = rms_scale(
            queries[:, j * HD : (j + 1) * HD].astype(jnp.float32), q_gain_ref[...]
        ).astype(jnp.bfloat16)

    def attend(owner, first):
        key_at = lax.broadcasted_iota(jnp.int32, (query_rows, segment), 1)
        query_at = lax.broadcasted_iota(jnp.int32, (query_rows, segment), 0)
        seen = jnp.where(
            key_at < cache_rows,
            (owner * cache_rows + key_at < limit_ref[...]).astype(jnp.int32),
            (
                owner * query_rows + key_at - cache_rows <= tok * query_rows + query_at
            ).astype(jnp.int32),
        )

        def one_head(j, _):
            scores = lax.dot_general(
                query_normed[j],
                keyval[owner, :, :HD],
                (((1,), (1,)), ((), ())),
                preferred_element_type=jnp.float32,
            )
            weights = jnp.where(seen > 0, jnp.exp(scores * HD ** (-0.5)), 0.0)
            sums = weights[:, :128]
            for i in range(1, segment // 128):
                sums = sums + weights[:, i * 128 : (i + 1) * 128]
            value = dot32(weights.astype(jnp.bfloat16), keyval[owner, :, HD:])
            weight_sum[j] = sums if first else weight_sum[j] + sums
            mixed[j] = value if first else mixed[j] + value
            return 0

        lax.fori_loop(0, local_heads, one_head, 0, unroll=2)

    attend(tok, True)
    arrive(2, 0, "z", lambda i, p: routing.at[tok, p, y])
    spread_out(3, 0, "y", routing.at[tok, :, y])
    arrive(1, 0, "core", lambda i, p: keyval.at[x * CORES + p])
    attend(x * CORES + 1 - core, False)
    arrive(3, 0, "y", lambda i, p: routing.at[tok, :, p])
    spread_out(4, 0, "x", routing.at[tok])
    arrive(0, 0, "x", lambda i, p: keyval.at[p * CORES + core])
    for i in range(1, nx):
        spread_out(1, i, "core", keyval.at[lax.rem(x + nx - i, nx) * CORES + core])
    for i in range(1, nx):
        attend(lax.rem(x + nx - i, nx) * CORES + core, False)
    arrive(4, 0, "x", lambda i, p: routing.at[p * CORES + core])
    for q in range(nx):
        spread_out(5, q, "core", routing.at[q * CORES + core])
    for i in range(1, nx):
        near = lax.rem(x + nx - i, nx) * CORES
        arrive(1, i, "core", lambda _, p: keyval.at[near + p])
        attend(near + 1 - core, False)
    for j in range(local_heads):
        attn[:, j * HD : (j + 1) * HD] = (
            mixed[j] / jnp.sum(weight_sum[j], axis=1, keepdims=True)
        ).astype(jnp.bfloat16)

    squares = []

    def project(k):
        c = columns[k]
        out_w_loads[k].wait()
        proj = dot32(attn[...], out_w[:, c]).astype(jnp.bfloat16)
        part[:, :, :, c] = proj.reshape(nz, ny, rows_out, step)
        send(6, k, "y", lambda p: part.at[:, p, :, c], lambda i: part_y.at[i - 1, :, :, c])

    def reduce_y(k):
        c = columns[k]
        arrive(6, k, "y", lambda i, p: part_y.at[i - 1, :, :, c])
        value = total(part[:, y, :, c], [part_y[i, :, :, c] for i in range(ny - 1)])
        sum_y[:, :, c] = value.astype(jnp.bfloat16)
        send(7, k, "z", lambda p: sum_y.at[p, :, c], lambda i: part_z.at[i - 1, :, c])

    def reduce_z(k):
        c = columns[k]
        arrive(7, k, "z", lambda i, p: part_z.at[i - 1, :, c])
        value = total(sum_y[z, :, c], [part_z[i, :, c] for i in range(nz - 1)])
        value = value + residual_ref[:, c].astype(jnp.float32)
        hidden[:, c] = value
        squares.append(jnp.sum(value * value, axis=1, keepdims=True))
        rows[tok, z, y, :, c] = (value * gain_ref[:, c]).astype(jnp.bfloat16)
        if k == CHUNKS - 1:
            scale = lax.rsqrt(sum(squares) / width + EPSILON)
            high = scale.astype(jnp.bfloat16).astype(jnp.float32)
            lane = lax.broadcasted_iota(jnp.int32, (rows_out, 128), 1)
            both = jnp.where(lane == 0, high, jnp.where(lane == 1, scale - high, 0.0))
            rows[tok, z, y, :, pl.ds(width, 128)] = both.astype(jnp.bfloat16)
        spread_out(8, k, "z", rows.at[tok, z, y, :, spans[k]])

    def gather_z(k):
        c = spans[k]
        arrive(8, k, "z", lambda i, p: rows.at[tok, p, y, :, c])
        spread_out(9, k, "y", rows.at[tok, :, y, :, c])

    def gather_y(k):
        c = spans[k]
        arrive(9, k, "y", lambda i, p: rows.at[tok, :, p, :, c])
        spread_out(10, k, "x", rows.at[tok, :, :, :, c])
        spread_out(11, k, "core", rows.at[tok, :, :, :, c])

    def gather_x(k):
        c = spans[k]
        arrive(10, k, "x", lambda i, p: rows.at[p * CORES + core, :, :, :, c])
        for i in range(1, nx):
            far = lax.rem(x + nx - i, nx) * CORES + core
            spread_out(11 + i, k, "core", rows.at[far, :, :, :, c])

    def up(k):
        c = spans[k]
        arrive(11, k, "core", lambda i, p: rows.at[x * CORES + p, :, :, :, c])
        for i in range(1, nx):
            near = lax.rem(x + nx - i, nx) * CORES
            arrive(11 + i, k, "core", lambda _, p: rows.at[near + p, :, :, :, c])
        picked = dot32(select[...], rows[:, :, :, :, c].reshape(tokens, -1))
        gate_up_loads[k].wait()
        both = dot32(picked[:, :step].astype(jnp.bfloat16), gate_up[columns[k], :])
        both = both if k == 0 else acc[...] + both
        if k == CHUNKS - 1:
            both = both * jnp.sum(picked[:, step:], axis=1, keepdims=True)
        acc[...] = both

    def place_rows():
        for q in range(nx):
            arrive(5, q, "core", lambda i, p: routing.at[q * CORES + p])
        own = (head * tok_count + tok).astype(jnp.float32)
        flat = routing[...].reshape(tokens, 256).astype(jnp.float32)
        named = flat[:, :128] == own
        chosen = jnp.sum(jnp.where(named, 1.0, 0.0), axis=1, keepdims=True)
        scale = jnp.sum(jnp.where(named, flat[:, 128:], 0.0), axis=1, keepdims=True)
        here = lax.broadcasted_iota(jnp.int32, (tokens, tokens), 0)
        there = lax.broadcasted_iota(jnp.int32, (tokens, tokens), 1)
        earlier = (there < here) & (there >= here - lax.rem(here, rows_out))
        before = dot32(
            jnp.where(earlier, 1.0, 0.0).astype(jnp.bfloat16),
            jnp.broadcast_to(chosen, (tokens, 128)).astype(jnp.bfloat16),
        )[:, :1]
        at = lax.broadcasted_iota(jnp.int32, (tokens, 1), 0)
        start = lax.div(at, rows_out) * capacity
        place = jnp.where(chosen > 0.0, start.astype(jnp.float32) + before, -1.0)
        slot = lax.broadcasted_iota(jnp.int32, (tokens, slots), 1)
        hit = slot == place.astype(jnp.int32)
        spread[...] = jnp.where(hit, scale, 0.0).astype(jnp.bfloat16)
        select[...] = jnp.where(hit, 1.0, 0.0).T.astype(jnp.bfloat16)

    def first_up(k):
        if k == 0:
            place_rows()
        gather_z(k)

    wavefront([project, reduce_y, reduce_z, first_up, gather_y, gather_x, up])

    gate = acc[:, :hidden_units]
    active[...] = (jax.nn.silu(gate) * acc[:, hidden_units:]).astype(jnp.bfloat16)

    base = 11 + nx

    def give(k):
        c = columns[k]
        down_loads[k].wait()
        expert_out = dot32(active[...], down[:, c]).astype(jnp.bfloat16)
        weighted = dot32(spread[...], expert_out).astype(jnp.bfloat16)
        share[:, :, :, :, :, c] = weighted.reshape(nx, CORES, nz, ny, rows_out, step)
        send(
            base,
            k,
            "core",
            lambda p: share.at[:, p, :, :, :, c],
            lambda i: in_core.at[:, :, :, :, c],
        )

    def return_core(k):
        c = columns[k]
        arrive(base, k, "core", lambda i, p: in_core.at[:, :, :, :, c])
        value = total(share[:, core, :, :, :, c], [in_core[:, :, :, :, c]])
        sum_core[:, :, :, :, c] = value.astype(jnp.bfloat16)
        if k % 2 == 0:
            send(
                base + 1,
                k,
                "x",
                lambda p: sum_core.at[p, :, :, :, c],
                lambda i: in_ax.at[i - 1, :, :, :, c],
            )
        else:
            send(
                base + 1,
                k,
                "y",
                lambda p: sum_core.at[:, :, p, :, c],
                lambda i: in_ay.at[i - 1, :, :, :, c],
            )

    def return_first(k):
        c = columns[k]
        if k % 2 == 0:
            arrive(base + 1, k, "x", lambda i, p: in_ax.at[i - 1, :, :, :, c])
            value = total(
                sum_core[x, :, :, :, c], [in_ax[i, :, :, :, c] for i in range(nx - 1)]
            )
            sum_ax[:, :, :, c] = value.astype(jnp.bfloat16)
            send(
                base + 2,
                k,
                "y",
                lambda p: sum_ax.at[:, p, :, c],
                lambda i: in_by.at[i - 1, :, :, c],
            )
        else:
            arrive(base + 1, k, "y", lambda i, p: in_ay.at[i - 1, :, :, :, c])
            value = total(
                sum_core[:, :, y, :, c], [in_ay[i, :, :, :, c] for i in range(ny - 1)]
            )
            sum_ay[:, :, :, c] = value.astype(jnp.bfloat16)
            send(
                base + 2,
                k,
                "x",
                lambda p: sum_ay.at[p, :, :, c],
                lambda i: in_bx.at[i - 1, :, :, c],
            )

    def return_second(k):
        c = columns[k]
        if k % 2 == 0:
            arrive(base + 2, k, "y", lambda i, p: in_by.at[i - 1, :, :, c])
            value = total(sum_ax[:, y, :, c], [in_by[i, :, :, c] for i in range(ny - 1)])
        else:
            arrive(base + 2, k, "x", lambda i, p: in_bx.at[i - 1, :, :, c])
            value = total(sum_ay[x, :, :, c], [in_bx[i, :, :, c] for i in range(nx - 1)])
        sum_b[:, :, c] = value.astype(jnp.bfloat16)
        send(base + 3, k, "z", lambda p: sum_b.at[p, :, c], lambda i: in_z.at[i - 1, :, c])

    def return_z(k):
        c = columns[k]
        arrive(base + 3, k, "z", lambda i, p: in_z.at[i - 1, :, c])
        value = total(sum_b[z, :, c], [in_z[i, :, c] for i in range(nz - 1)])
        result_ref[:, c] = (hidden[:, c] + value).astype(jnp.bfloat16)

    wavefront([give, return_core, return_first, return_second, return_z])
    for copy in sends:
        copy.wait_send()


def routed_layer(
    queries,
    cache,
    new_kv,
    q_gain,
    k_gain,
    out_weight,
    residual,
    norm_gain,
    expert_ids,
    combine_weight,
    prefix_len,
    w_gate_up,
    w_down,
):
    head_count = lax.axis_size("head")
    tok_count = lax.axis_size("tok")
    nz, ny, nx = DEPTH, head_count // DEPTH, tok_count // CORES
    width = out_weight.shape[1]
    rows_out, topk = expert_ids.shape
    experts_all = head_count * tok_count
    tokens = rows_out * experts_all
    capacity = max(2, 2 * rows_out * topk // experts_all)
    slots = experts_all * capacity
    hidden_units = w_down.shape[1]

    b16, f32 = jnp.bfloat16, jnp.float32
    vmem = pl.BlockSpec(memory_space=pltpu.VMEM)
    hbm = pl.BlockSpec(memory_space=pl.ANY)
    stages = 15 + nx
    query_rows = queries.shape[0]
    heads = queries.shape[1] // HD
    segment = cache.shape[1] + query_rows
    widest = max(nz, ny, nx, CORES) - 1
    scratch = [
        pltpu.VMEM(queries.shape, b16),
        pltpu.VMEM((tok_count, segment, 2 * HD), b16),
        pltpu.VMEM((heads, query_rows, HD), b16),
        pltpu.VMEM((heads, query_rows, HD), f32),
        pltpu.VMEM((heads, query_rows, 128), f32),
        pltpu.VMEM(queries.shape, b16),
        pltpu.VMEM((tok_count, nz, ny, rows_out, 256), b16),
        pltpu.VMEM((slots, tokens), b16),
        pltpu.VMEM((tokens, slots), b16),
        pltpu.VMEM(out_weight.shape, b16),
        pltpu.VMEM(w_gate_up.shape[1:], b16),
        pltpu.VMEM(w_down.shape[1:], b16),
        pltpu.VMEM((nz, ny, rows_out, width), b16),
        pltpu.VMEM((ny - 1, nz, rows_out, width), b16),
        pltpu.VMEM((nz, rows_out, width), b16),
        pltpu.VMEM((nz - 1, rows_out, width), b16),
        pltpu.VMEM((rows_out, width), f32),
        pltpu.VMEM((tok_count, nz, ny, rows_out, width + 128), b16),
        pltpu.VMEM((slots, 2 * hidden_units), f32),
        pltpu.VMEM((slots, hidden_units), b16),
        pltpu.VMEM((nx, CORES, nz, ny, rows_out, width), b16),
        pltpu.VMEM((nx, nz, ny, rows_out, width), b16),
        pltpu.VMEM((nx, nz, ny, rows_out, width), b16),
        pltpu.VMEM((nx - 1, nz, ny, rows_out, width), b16),
        pltpu.VMEM((ny - 1, nx, nz, rows_out, width), b16),
        pltpu.VMEM((nz, ny, rows_out, width), b16),
        pltpu.VMEM((nx, nz, rows_out, width), b16),
        pltpu.VMEM((nx - 1, nz, rows_out, width), b16),
        pltpu.VMEM((ny - 1, nz, rows_out, width), b16),
        pltpu.VMEM((nz, rows_out, width), b16),
        pltpu.VMEM((nz - 1, rows_out, width), b16),
        pltpu.SemaphoreType.DMA((3 + 3 * CHUNKS,)),
        pltpu.SemaphoreType.DMA((stages, CHUNKS, widest)),
        pltpu.SemaphoreType.DMA((stages, CHUNKS, widest)),
    ]
    return pl.pallas_call(
        functools.partial(layer_kernel, (nz, ny, nx, capacity)),
        out_shape=jax.ShapeDtypeStruct((rows_out, width), b16),
        in_specs=[hbm] * 3 + [vmem] * 3 + [hbm] + [vmem] * 4 + [hbm] * 2,
        out_specs=vmem,
        scratch_shapes=scratch,
        compiler_params=pltpu.CompilerParams(
            collective_id=0, has_side_effects=True, vmem_limit_bytes=VMEM_BYTES
        ),
    )(
        queries,
        cache,
        new_kv,
        q_gain.reshape(1, HD),
        k_gain.reshape(1, HD),
        prefix_len.reshape(1, 1),
        out_weight,
        residual,
        norm_gain.reshape(1, width),
        expert_ids,
        combine_weight,
        w_gate_up,
        w_down,
    )


def fits(tokens, width, experts):
    return 12 * tokens * width <= VMEM_BYTES // 2 and experts <= 256


def per_device(
    queries,
    cache,
    new_kv,
    q_gain,
    k_gain,
    out_weight,
    residual,
    norm_gain,
    expert_ids,
    combine_weight,
    prefix_len,
    w_gate_up,
    w_down,
):
    head_count = lax.axis_size("head")
    tok_count = lax.axis_size("tok")
    query_rows = queries.shape[0]
    if fits(query_rows * tok_count, out_weight.shape[1], head_count * tok_count):
        return routed_layer(
            queries,
            cache,
            new_kv,
            q_gain,
            k_gain,
            out_weight,
            residual,
            norm_gain,
            expert_ids,
            combine_weight,
            prefix_len,
            w_gate_up,
            w_down,
        )
    local_heads = queries.shape[1] // HD
    cache_rows = cache.shape[1]
    segment = cache_rows + query_rows
    kv_index = lax.axis_index("head") * local_heads // (HEADS // KV_HEADS)
    query_normed = rms_scale(
        queries.reshape(query_rows, local_heads, HD).astype(jnp.float32), q_gain
    ).astype(jnp.bfloat16)
    own_block = jnp.concatenate(
        [
            lax.dynamic_index_in_dim(cache, kv_index, 0, keepdims=False),
            lax.dynamic_index_in_dim(new_kv, kv_index, 0, keepdims=False),
        ],
        axis=0,
    )
    key_part = rms_scale(own_block[:, :HD].astype(jnp.float32), k_gain).astype(jnp.bfloat16)
    key_block = jnp.concatenate([key_part, own_block[:, HD:]], axis=1)
    query_position = lax.axis_index("tok") * query_rows + jnp.arange(query_rows, dtype=jnp.int32)
    limit = prefix_len[0]
    piece = lax.all_gather(key_block, "tok", axis=0, tiled=True)
    position = jnp.arange(piece.shape[0], dtype=jnp.int32)
    shard = position // segment
    offset = position % segment
    in_cache = offset < cache_rows
    cache_position = shard * cache_rows + offset
    span_position = shard * query_rows + offset - cache_rows
    visible = jnp.where(
        in_cache[None, :],
        (cache_position < limit)[None, :],
        span_position[None, :] <= query_position[:, None],
    )
    scores = jnp.einsum(
        "qhd,kd->qhk", query_normed, piece[:, :HD], preferred_element_type=jnp.float32
    ) * HD ** (-0.5)
    weights = jnp.where(visible[:, None, :], jnp.exp(scores), 0.0)
    accum = jnp.einsum(
        "qhk,kd->qhd",
        weights.astype(jnp.bfloat16),
        piece[:, HD:],
        preferred_element_type=jnp.float32,
    )
    total = jnp.sum(weights, axis=2)
    accum, total = (accum, total)
    attn = (accum / total[:, :, None]).astype(jnp.bfloat16).reshape(query_rows, local_heads * HD)
    rows_out = query_rows // head_count
    full_proj = lax.psum(
        jnp.dot(attn, out_weight, preferred_element_type=jnp.float32).astype(jnp.bfloat16), "head"
    ).astype(jnp.float32)
    attn_proj = lax.dynamic_slice_in_dim(full_proj, lax.axis_index("head") * rows_out, rows_out, 0)
    hidden = residual.astype(jnp.float32) + attn_proj
    normed = rms_scale(hidden, norm_gain).astype(jnp.bfloat16)
    width = normed.shape[1]
    experts_all = head_count * tok_count
    topk = expert_ids.shape[1]
    capacity = max(2, 2 * rows_out * topk // experts_all)
    flat_ids = expert_ids.reshape(-1)
    onehot = (flat_ids[:, None] == jnp.arange(experts_all, dtype=jnp.int32)[None, :]).astype(
        jnp.int32
    )
    before = jnp.cumsum(onehot, axis=0) - onehot
    slot_index = jnp.sum(before * onehot, axis=1)
    target = (flat_ids * capacity + slot_index).reshape(rows_out, topk)
    matches = (
        target[:, :, None] == jnp.arange(experts_all * capacity, dtype=jnp.int32)[None, None, :]
    )
    placing = jnp.sum(matches.astype(jnp.int32), axis=1).astype(jnp.bfloat16)
    mixing = jnp.sum(
        jnp.where(matches, combine_weight.astype(jnp.float32)[:, :, None], 0.0), axis=1
    ).astype(jnp.bfloat16)
    outgoing = jnp.einsum("rs,rd->sd", placing, normed, preferred_element_type=jnp.float32).astype(
        jnp.bfloat16
    )
    outgoing = outgoing.reshape(experts_all, capacity, width)
    returned = lax.all_to_all(
        expert_block(
            lax.all_to_all(outgoing, ("head", "tok"), split_axis=0, concat_axis=0, tiled=True),
            w_gate_up[0],
            w_down[0],
        ),
        ("head", "tok"),
        split_axis=0,
        concat_axis=0,
        tiled=True,
    )
    back_rows = returned.reshape(experts_all * capacity, width)
    expert_sum = jnp.dot(mixing, back_rows, preferred_element_type=jnp.float32)
    return (hidden + expert_sum).astype(jnp.bfloat16)

def solution(mesh):
    placed = (
        P("tok", "head"),
        P(None, "tok", None),
        P(None, "tok", None),
        P(),
        P(),
        P("head", None),
        P(("tok", "head"), None),
        P(),
        P(("tok", "head"), None),
        P(("tok", "head"), None),
        P(),
        P(("head", "tok"), None, None),
        P(("head", "tok"), None, None),
    )
    return jax.shard_map(
        per_device, mesh=mesh, in_specs=placed, out_specs=P(("tok", "head"), None), check_vma=False
    )
```

```python
import functools

import jax
import jax.numpy as jnp
from jax import lax
from jax.experimental import pallas as pl
from jax.experimental.pallas import tpu as pltpu
from jax.sharding import PartitionSpec as P

HEADS = 64
KV_HEADS = 4
HD = 128


EPSILON = 1e-06


def rms_scale(values, gain):
    mean_square = jnp.mean(values * values, axis=-1, keepdims=True)
    return values * lax.rsqrt(mean_square + EPSILON) * gain


def expert_block(inputs, gate_up, down_proj):
    width = down_proj.shape[1]
    hidden_units = down_proj.shape[0]
    flat_rows = inputs.reshape(-1, width)
    both = jnp.dot(flat_rows, gate_up, preferred_element_type=jnp.float32)
    active = (jax.nn.silu(both[:, :hidden_units]) * both[:, hidden_units:]).astype(jnp.bfloat16)
    result = jnp.dot(active, down_proj, preferred_element_type=jnp.float32).astype(jnp.bfloat16)
    return result.reshape(inputs.shape)


DEPTH = 4
CORES = 2
CHUNKS = 8
GROUP = 4
FLIGHT = 2
VMEM_BYTES = 60 * 2**20
MESH = pl.DeviceIdType.MESH


def dot32(a, b):
    return jnp.dot(a, b, preferred_element_type=jnp.float32)


def layer_kernel(
    dims,
    queries_hbm,
    cache_hbm,
    new_kv_hbm,
    q_gain_ref,
    k_gain_ref,
    limit_ref,
    out_weight_hbm,
    residual_ref,
    gain_ref,
    ids_ref,
    combine_ref,
    gate_up_hbm,
    down_hbm,
    result_ref,
    queries,
    keyval,
    query_normed,
    mixed,
    weight_sum,
    attn,
    routing,
    select,
    spread,
    out_w,
    gate_up,
    down,
    part,
    part_y,
    sum_y,
    part_z,
    hidden,
    rows,
    acc,
    active,
    share,
    in_core,
    sum_core,
    in_ax,
    in_ay,
    sum_ax,
    sum_ay,
    in_bx,
    in_by,
    sum_b,
    in_z,
    load_sem,
    send_sem,
    recv_sem,
):
    nz, ny, nx, capacity = dims
    head, tok = lax.axis_index("head"), lax.axis_index("tok")
    z, y = lax.div(head, ny), lax.rem(head, ny)
    x, core = lax.div(tok, CORES), lax.rem(tok, CORES)
    tok_count = nx * CORES
    width = hidden.shape[1]
    rows_out = hidden.shape[0]
    step = width // CHUNKS
    slots, tokens = select.shape
    topk = ids_ref.shape[0]
    hidden_units = down.shape[0]
    query_rows = queries.shape[0]
    local_heads = queries.shape[1] // HD
    cache_rows = cache_hbm.shape[1]
    segment = keyval.shape[1]
    columns = [pl.ds(k * step, step) for k in range(CHUNKS)]
    spans = columns[:-1] + [pl.ds(width - step, step + 128)]

    axes = {
        "z": (nz, z, lambda p: (p * ny + y, tok)),
        "y": (ny, y, lambda p: (z * ny + p, tok)),
        "x": (nx, x, lambda p: (head, p * CORES + core)),
        "core": (CORES, core, lambda p: (head, x * CORES + p)),
    }

    loads = []

    def load(src, dst):
        copy = pltpu.make_async_copy(src, dst, load_sem.at[len(loads)])
        copy.start()
        loads.append(copy)
        return copy

    kv_index = lax.div(head * local_heads, HEADS // KV_HEADS)
    kv_loads = [
        load(cache_hbm.at[kv_index], keyval.at[tok, pl.ds(0, cache_rows)]),
        load(new_kv_hbm.at[kv_index], keyval.at[tok, pl.ds(cache_rows, query_rows)]),
    ]
    query_load = load(queries_hbm, queries)
    out_w_loads = [load(out_weight_hbm.at[:, c], out_w.at[:, c]) for c in columns]
    gate_up_loads = [load(gate_up_hbm.at[0, c, :], gate_up.at[c, :]) for c in columns]
    down_loads = [load(down_hbm.at[0, :, c], down.at[:, c]) for c in columns]

    barrier = pltpu.get_barrier_semaphore()
    greeted = 0
    for n, me, device in axes.values():
        for i in range(1, n):
            pl.semaphore_signal(
                barrier, inc=1, device_id=device(lax.rem(me + i, n)), device_id_type=MESH
            )
            greeted += 1

    sends = []

    def send(stage, k, axis, source, target):
        n, me, device = axes[axis]
        for i in range(1, n):
            peer = lax.rem(me + i, n)
            copy = pltpu.make_async_remote_copy(
                src_ref=source(peer),
                dst_ref=target(i),
                send_sem=send_sem.at[stage, k, i - 1],
                recv_sem=recv_sem.at[stage, k, i - 1],
                device_id=device(peer),
                device_id_type=MESH,
            )
            copy.start()
            sends.append(copy)

    def spread_out(stage, k, axis, place):
        send(stage, k, axis, lambda _: place, lambda _: place)

    def arrive(stage, k, axis, region):
        n, me, device = axes[axis]
        for i in range(1, n):
            peer = lax.rem(me + n - i, n)
            place = region(i, peer)
            pltpu.make_async_remote_copy(
                src_ref=place,
                dst_ref=place,
                send_sem=send_sem.at[stage, k, i - 1],
                recv_sem=recv_sem.at[stage, k, i - 1],
                device_id=device(peer),
                device_id_type=MESH,
            ).wait_recv()

    def total(first, others):
        value = first.astype(jnp.float32)
        for other in others:
            value = value + other.astype(jnp.float32)
        return value

    def wavefront(stages):
        for turn in range(CHUNKS + FLIGHT * (len(stages) - 1)):
            for place in reversed(range(len(stages))):
                if 0 <= turn - FLIGHT * place < CHUNKS:
                    stages[place](turn - FLIGHT * place)

    lane = lax.broadcasted_iota(jnp.int32, (topk, 128), 1)
    turned = jnp.where(lane == lax.broadcasted_iota(jnp.int32, (topk, 128), 0), 1.0, 0.0)
    empty = lax.broadcasted_iota(jnp.int32, (rows_out, 128), 1) >= topk

    def by_row(ref):
        return lax.dot_general(
            ref[...].astype(jnp.float32),
            turned,
            (((0,), (0,)), ((), ())),
            preferred_element_type=jnp.float32,
        )

    routing[tok, z, y, :, :128] = jnp.where(empty, -1.0, by_row(ids_ref)).astype(jnp.bfloat16)
    routing[tok, z, y, :, 128:] = by_row(combine_ref).astype(jnp.bfloat16)
    for copy in kv_loads:
        copy.wait()
    keyval[tok, :, :HD] = rms_scale(
        keyval[tok, :, :HD].astype(jnp.float32), k_gain_ref[...]
    ).astype(jnp.bfloat16)
    pl.semaphore_wait(barrier, greeted)
    spread_out(0, 0, "x", keyval.at[tok])
    spread_out(1, 0, "core", keyval.at[tok])
    spread_out(2, 0, "z", routing.at[tok, z, y])
    query_load.wait()
    for j in range(local_heads):
        query_normed[j * query_rows : (j + 1) * query_rows] = rms_scale(
            queries[:, j * HD : (j + 1) * HD].astype(jnp.float32), q_gain_ref[...]
        ).astype(jnp.bfloat16)

    def attend(owner, first):
        key_at = lax.broadcasted_iota(jnp.int32, (query_rows, segment), 1)
        query_at = lax.broadcasted_iota(jnp.int32, (query_rows, segment), 0)
        seen = jnp.where(
            key_at < cache_rows,
            (owner * cache_rows + key_at < limit_ref[...]).astype(jnp.int32),
            (
                owner * query_rows + key_at - cache_rows <= tok * query_rows + query_at
            ).astype(jnp.int32),
        )

        for j in range(0, local_heads * query_rows, GROUP * query_rows):
            part_rows = pl.ds(j, GROUP * query_rows)
            scores = lax.dot_general(
                query_normed[part_rows],
                keyval[owner, :, :HD],
                (((1,), (1,)), ((), ())),
                preferred_element_type=jnp.float32,
            )
            scores = (scores * HD ** (-0.5)).reshape(GROUP, query_rows, segment)
            weights = jnp.where(seen[None] > 0, jnp.exp(scores), 0.0)
            weights = weights.reshape(GROUP * query_rows, segment)
            sums = weights[:, :128]
            for i in range(1, segment // 128):
                sums = sums + weights[:, i * 128 : (i + 1) * 128]
            value = dot32(weights.astype(jnp.bfloat16), keyval[owner, :, HD:])
            weight_sum[part_rows] = sums if first else weight_sum[part_rows] + sums
            mixed[part_rows] = value if first else mixed[part_rows] + value

    attend(tok, True)
    arrive(2, 0, "z", lambda i, p: routing.at[tok, p, y])
    spread_out(3, 0, "y", routing.at[tok, :, y])
    arrive(1, 0, "core", lambda i, p: keyval.at[x * CORES + p])
    attend(x * CORES + 1 - core, False)
    arrive(3, 0, "y", lambda i, p: routing.at[tok, :, p])
    spread_out(4, 0, "x", routing.at[tok])
    arrive(0, 0, "x", lambda i, p: keyval.at[p * CORES + core])
    for i in range(1, nx):
        spread_out(1, i, "core", keyval.at[lax.rem(x + nx - i, nx) * CORES + core])
    for i in range(1, nx):
        attend(lax.rem(x + nx - i, nx) * CORES + core, False)
    arrive(4, 0, "x", lambda i, p: routing.at[p * CORES + core])
    for q in range(nx):
        spread_out(5, q, "core", routing.at[q * CORES + core])
    for i in range(1, nx):
        near = lax.rem(x + nx - i, nx) * CORES
        arrive(1, i, "core", lambda _, p: keyval.at[near + p])
        attend(near + 1 - core, False)
    for j in range(local_heads):
        mine = pl.ds(j * query_rows, query_rows)
        attn[:, j * HD : (j + 1) * HD] = (
            mixed[mine] / jnp.sum(weight_sum[mine], axis=1, keepdims=True)
        ).astype(jnp.bfloat16)

    squares = []

    def project(k):
        c = columns[k]
        out_w_loads[k].wait()
        proj = dot32(attn[...], out_w[:, c]).astype(jnp.bfloat16)
        part[:, :, :, c] = proj.reshape(nz, ny, rows_out, step)
        send(6, k, "y", lambda p: part.at[:, p, :, c], lambda i: part_y.at[i - 1, :, :, c])
        if k == FLIGHT - 1:
            place_rows()

    def reduce_y(k):
        c = columns[k]
        arrive(6, k, "y", lambda i, p: part_y.at[i - 1, :, :, c])
        value = total(part[:, y, :, c], [part_y[i, :, :, c] for i in range(ny - 1)])
        sum_y[:, :, c] = value.astype(jnp.bfloat16)
        send(7, k, "z", lambda p: sum_y.at[p, :, c], lambda i: part_z.at[i - 1, :, c])

    def reduce_z(k):
        c = columns[k]
        arrive(7, k, "z", lambda i, p: part_z.at[i - 1, :, c])
        value = total(sum_y[z, :, c], [part_z[i, :, c] for i in range(nz - 1)])
        value = value + residual_ref[:, c].astype(jnp.float32)
        hidden[:, c] = value
        squares.append(jnp.sum(value * value, axis=1, keepdims=True))
        rows[tok, z, y, :, c] = (value * gain_ref[:, c]).astype(jnp.bfloat16)
        if k == CHUNKS - 1:
            scale = lax.rsqrt(sum(squares) / width + EPSILON)
            high = scale.astype(jnp.bfloat16).astype(jnp.float32)
            lane = lax.broadcasted_iota(jnp.int32, (rows_out, 128), 1)
            both = jnp.where(lane == 0, high, jnp.where(lane == 1, scale - high, 0.0))
            rows[tok, z, y, :, pl.ds(width, 128)] = both.astype(jnp.bfloat16)
        spread_out(8, k, "z", rows.at[tok, z, y, :, spans[k]])

    def gather_z(k):
        c = spans[k]
        arrive(8, k, "z", lambda i, p: rows.at[tok, p, y, :, c])
        spread_out(9, k, "y", rows.at[tok, :, y, :, c])

    def gather_y(k):
        c = spans[k]
        arrive(9, k, "y", lambda i, p: rows.at[tok, :, p, :, c])
        spread_out(10, k, "x", rows.at[tok, :, :, :, c])
        spread_out(11, k, "core", rows.at[tok, :, :, :, c])

    def gather_x(k):
        c = spans[k]
        arrive(10, k, "x", lambda i, p: rows.at[p * CORES + core, :, :, :, c])
        for i in range(1, nx):
            far = lax.rem(x + nx - i, nx) * CORES + core
            spread_out(11 + i, k, "core", rows.at[far, :, :, :, c])

    def up(k):
        c = spans[k]
        arrive(11, k, "core", lambda i, p: rows.at[x * CORES + p, :, :, :, c])
        for i in range(1, nx):
            near = lax.rem(x + nx - i, nx) * CORES
            arrive(11 + i, k, "core", lambda _, p: rows.at[near + p, :, :, :, c])
        picked = dot32(select[...], rows[:, :, :, :, c].reshape(tokens, -1))
        gate_up_loads[k].wait()
        both = dot32(picked[:, :step].astype(jnp.bfloat16), gate_up[columns[k], :])
        both = both if k == 0 else acc[...] + both
        if k == CHUNKS - 1:
            both = both * jnp.sum(picked[:, step:], axis=1, keepdims=True)
        acc[...] = both

    def place_rows():
        for q in range(nx):
            arrive(5, q, "core", lambda i, p: routing.at[q * CORES + p])
        own = (head * tok_count + tok).astype(jnp.float32)
        flat = routing[...].reshape(tokens, 256).astype(jnp.float32)
        named = flat[:, :128] == own
        chosen = jnp.sum(jnp.where(named, 1.0, 0.0), axis=1, keepdims=True)
        scale = jnp.sum(jnp.where(named, flat[:, 128:], 0.0), axis=1, keepdims=True)
        here = lax.broadcasted_iota(jnp.int32, (tokens, tokens), 0)
        there = lax.broadcasted_iota(jnp.int32, (tokens, tokens), 1)
        earlier = (there < here) & (there >= here - lax.rem(here, rows_out))
        before = dot32(
            jnp.where(earlier, 1.0, 0.0).astype(jnp.bfloat16),
            jnp.broadcast_to(chosen, (tokens, 128)).astype(jnp.bfloat16),
        )[:, :1]
        at = lax.broadcasted_iota(jnp.int32, (tokens, 1), 0)
        start = lax.div(at, rows_out) * capacity
        place = jnp.where(chosen > 0.0, start.astype(jnp.float32) + before, -1.0)
        slot = lax.broadcasted_iota(jnp.int32, (tokens, slots), 1)
        hit = slot == place.astype(jnp.int32)
        spread[...] = jnp.where(hit, scale, 0.0).astype(jnp.bfloat16)
        select[...] = jnp.where(hit, 1.0, 0.0).T.astype(jnp.bfloat16)

    wavefront([project, reduce_y, reduce_z, gather_z, gather_y, gather_x, up])

    gate = acc[:, :hidden_units]
    active[...] = (jax.nn.silu(gate) * acc[:, hidden_units:]).astype(jnp.bfloat16)

    base = 11 + nx

    def give(k):
        c = columns[k]
        down_loads[k].wait()
        expert_out = dot32(active[...], down[:, c]).astype(jnp.bfloat16)
        weighted = dot32(spread[...], expert_out).astype(jnp.bfloat16)
        share[:, :, :, :, :, c] = weighted.reshape(nx, CORES, nz, ny, rows_out, step)
        send(
            base,
            k,
            "core",
            lambda p: share.at[:, p, :, :, :, c],
            lambda i: in_core.at[:, :, :, :, c],
        )

    def return_core(k):
        c = columns[k]
        arrive(base, k, "core", lambda i, p: in_core.at[:, :, :, :, c])
        value = total(share[:, core, :, :, :, c], [in_core[:, :, :, :, c]])
        sum_core[:, :, :, :, c] = value.astype(jnp.bfloat16)
        if k % 2 == 0:
            send(
                base + 1,
                k,
                "x",
                lambda p: sum_core.at[p, :, :, :, c],
                lambda i: in_ax.at[i - 1, :, :, :, c],
            )
        else:
            send(
                base + 1,
                k,
                "y",
                lambda p: sum_core.at[:, :, p, :, c],
                lambda i: in_ay.at[i - 1, :, :, :, c],
            )

    def return_first(k):
        c = columns[k]
        if k % 2 == 0:
            arrive(base + 1, k, "x", lambda i, p: in_ax.at[i - 1, :, :, :, c])
            value = total(
                sum_core[x, :, :, :, c], [in_ax[i, :, :, :, c] for i in range(nx - 1)]
            )
            sum_ax[:, :, :, c] = value.astype(jnp.bfloat16)
            send(
                base + 2,
                k,
                "y",
                lambda p: sum_ax.at[:, p, :, c],
                lambda i: in_by.at[i - 1, :, :, c],
            )
        else:
            arrive(base + 1, k, "y", lambda i, p: in_ay.at[i - 1, :, :, :, c])
            value = total(
                sum_core[:, :, y, :, c], [in_ay[i, :, :, :, c] for i in range(ny - 1)]
            )
            sum_ay[:, :, :, c] = value.astype(jnp.bfloat16)
            send(
                base + 2,
                k,
                "x",
                lambda p: sum_ay.at[p, :, :, c],
                lambda i: in_bx.at[i - 1, :, :, c],
            )

    def return_second(k):
        c = columns[k]
        if k % 2 == 0:
            arrive(base + 2, k, "y", lambda i, p: in_by.at[i - 1, :, :, c])
            value = total(sum_ax[:, y, :, c], [in_by[i, :, :, c] for i in range(ny - 1)])
        else:
            arrive(base + 2, k, "x", lambda i, p: in_bx.at[i - 1, :, :, c])
            value = total(sum_ay[x, :, :, c], [in_bx[i, :, :, c] for i in range(nx - 1)])
        sum_b[:, :, c] = value.astype(jnp.bfloat16)
        send(base + 3, k, "z", lambda p: sum_b.at[p, :, c], lambda i: in_z.at[i - 1, :, c])

    def return_z(k):
        c = columns[k]
        arrive(base + 3, k, "z", lambda i, p: in_z.at[i - 1, :, c])
        value = total(sum_b[z, :, c], [in_z[i, :, c] for i in range(nz - 1)])
        result_ref[:, c] = (hidden[:, c] + value).astype(jnp.bfloat16)

    wavefront([give, return_core, return_first, return_second, return_z])
    for copy in sends:
        copy.wait_send()


def routed_layer(
    queries,
    cache,
    new_kv,
    q_gain,
    k_gain,
    out_weight,
    residual,
    norm_gain,
    expert_ids,
    combine_weight,
    prefix_len,
    w_gate_up,
    w_down,
):
    head_count = lax.axis_size("head")
    tok_count = lax.axis_size("tok")
    nz, ny, nx = DEPTH, head_count // DEPTH, tok_count // CORES
    width = out_weight.shape[1]
    rows_out, topk = expert_ids.shape
    experts_all = head_count * tok_count
    tokens = rows_out * experts_all
    capacity = max(2, 2 * rows_out * topk // experts_all)
    slots = experts_all * capacity
    hidden_units = w_down.shape[1]

    b16, f32 = jnp.bfloat16, jnp.float32
    vmem = pl.BlockSpec(memory_space=pltpu.VMEM)
    hbm = pl.BlockSpec(memory_space=pl.ANY)
    stages = 15 + nx
    query_rows = queries.shape[0]
    heads = queries.shape[1] // HD
    segment = cache.shape[1] + query_rows
    widest = max(nz, ny, nx, CORES) - 1
    scratch = [
        pltpu.VMEM(queries.shape, b16),
        pltpu.VMEM((tok_count, segment, 2 * HD), b16),
        pltpu.VMEM((heads * query_rows, HD), b16),
        pltpu.VMEM((heads * query_rows, HD), f32),
        pltpu.VMEM((heads * query_rows, 128), f32),
        pltpu.VMEM(queries.shape, b16),
        pltpu.VMEM((tok_count, nz, ny, rows_out, 256), b16),
        pltpu.VMEM((slots, tokens), b16),
        pltpu.VMEM((tokens, slots), b16),
        pltpu.VMEM(out_weight.shape, b16),
        pltpu.VMEM(w_gate_up.shape[1:], b16),
        pltpu.VMEM(w_down.shape[1:], b16),
        pltpu.VMEM((nz, ny, rows_out, width), b16),
        pltpu.VMEM((ny - 1, nz, rows_out, width), b16),
        pltpu.VMEM((nz, rows_out, width), b16),
        pltpu.VMEM((nz - 1, rows_out, width), b16),
        pltpu.VMEM((rows_out, width), f32),
        pltpu.VMEM((tok_count, nz, ny, rows_out, width + 128), b16),
        pltpu.VMEM((slots, 2 * hidden_units), f32),
        pltpu.VMEM((slots, hidden_units), b16),
        pltpu.VMEM((nx, CORES, nz, ny, rows_out, width), b16),
        pltpu.VMEM((nx, nz, ny, rows_out, width), b16),
        pltpu.VMEM((nx, nz, ny, rows_out, width), b16),
        pltpu.VMEM((nx - 1, nz, ny, rows_out, width), b16),
        pltpu.VMEM((ny - 1, nx, nz, rows_out, width), b16),
        pltpu.VMEM((nz, ny, rows_out, width), b16),
        pltpu.VMEM((nx, nz, rows_out, width), b16),
        pltpu.VMEM((nx - 1, nz, rows_out, width), b16),
        pltpu.VMEM((ny - 1, nz, rows_out, width), b16),
        pltpu.VMEM((nz, rows_out, width), b16),
        pltpu.VMEM((nz - 1, rows_out, width), b16),
        pltpu.SemaphoreType.DMA((3 + 3 * CHUNKS,)),
        pltpu.SemaphoreType.DMA((stages, CHUNKS, widest)),
        pltpu.SemaphoreType.DMA((stages, CHUNKS, widest)),
    ]
    return pl.pallas_call(
        functools.partial(layer_kernel, (nz, ny, nx, capacity)),
        out_shape=jax.ShapeDtypeStruct((rows_out, width), b16),
        in_specs=[hbm] * 3 + [vmem] * 3 + [hbm] + [vmem] * 4 + [hbm] * 2,
        out_specs=vmem,
        scratch_shapes=scratch,
        compiler_params=pltpu.CompilerParams(
            collective_id=0, has_side_effects=True, vmem_limit_bytes=VMEM_BYTES
        ),
    )(
        queries,
        cache,
        new_kv,
        q_gain.reshape(1, HD),
        k_gain.reshape(1, HD),
        prefix_len.reshape(1, 1),
        out_weight,
        residual,
        norm_gain.reshape(1, width),
        expert_ids.T,
        combine_weight.T,
        w_gate_up,
        w_down,
    )


def fits(tokens, width, experts, spans, heads):
    if spans > CORES * CHUNKS or heads % GROUP:
        return False
    return 12 * tokens * width <= VMEM_BYTES // 2 and experts <= 256


def per_device(
    queries,
    cache,
    new_kv,
    q_gain,
    k_gain,
    out_weight,
    residual,
    norm_gain,
    expert_ids,
    combine_weight,
    prefix_len,
    w_gate_up,
    w_down,
):
    head_count = lax.axis_size("head")
    tok_count = lax.axis_size("tok")
    query_rows = queries.shape[0]
    local_heads = queries.shape[1] // HD
    experts_all = head_count * tok_count
    tokens = query_rows * tok_count
    if fits(tokens, out_weight.shape[1], experts_all, tok_count, local_heads):
        return routed_layer(
            queries,
            cache,
            new_kv,
            q_gain,
            k_gain,
            out_weight,
            residual,
            norm_gain,
            expert_ids,
            combine_weight,
            prefix_len,
            w_gate_up,
            w_down,
        )
    cache_rows = cache.shape[1]
    segment = cache_rows + query_rows
    kv_index = lax.axis_index("head") * local_heads // (HEADS // KV_HEADS)
    query_normed = rms_scale(
        queries.reshape(query_rows, local_heads, HD).astype(jnp.float32), q_gain
    ).astype(jnp.bfloat16)
    own_block = jnp.concatenate(
        [
            lax.dynamic_index_in_dim(cache, kv_index, 0, keepdims=False),
            lax.dynamic_index_in_dim(new_kv, kv_index, 0, keepdims=False),
        ],
        axis=0,
    )
    key_part = rms_scale(own_block[:, :HD].astype(jnp.float32), k_gain).astype(jnp.bfloat16)
    key_block = jnp.concatenate([key_part, own_block[:, HD:]], axis=1)
    query_position = lax.axis_index("tok") * query_rows + jnp.arange(query_rows, dtype=jnp.int32)
    limit = prefix_len[0]
    piece = lax.all_gather(key_block, "tok", axis=0, tiled=True)
    position = jnp.arange(piece.shape[0], dtype=jnp.int32)
    shard = position // segment
    offset = position % segment
    in_cache = offset < cache_rows
    cache_position = shard * cache_rows + offset
    span_position = shard * query_rows + offset - cache_rows
    visible = jnp.where(
        in_cache[None, :],
        (cache_position < limit)[None, :],
        span_position[None, :] <= query_position[:, None],
    )
    scores = jnp.einsum(
        "qhd,kd->qhk", query_normed, piece[:, :HD], preferred_element_type=jnp.float32
    ) * HD ** (-0.5)
    weights = jnp.where(visible[:, None, :], jnp.exp(scores), 0.0)
    accum = jnp.einsum(
        "qhk,kd->qhd",
        weights.astype(jnp.bfloat16),
        piece[:, HD:],
        preferred_element_type=jnp.float32,
    )
    total = jnp.sum(weights, axis=2)
    accum, total = (accum, total)
    attn = (accum / total[:, :, None]).astype(jnp.bfloat16).reshape(query_rows, local_heads * HD)
    rows_out = query_rows // head_count
    full_proj = lax.psum(
        jnp.dot(attn, out_weight, preferred_element_type=jnp.float32).astype(jnp.bfloat16), "head"
    ).astype(jnp.float32)
    attn_proj = lax.dynamic_slice_in_dim(full_proj, lax.axis_index("head") * rows_out, rows_out, 0)
    hidden = residual.astype(jnp.float32) + attn_proj
    normed = rms_scale(hidden, norm_gain).astype(jnp.bfloat16)
    width = normed.shape[1]
    experts_all = head_count * tok_count
    topk = expert_ids.shape[1]
    capacity = max(2, 2 * rows_out * topk // experts_all)
    flat_ids = expert_ids.reshape(-1)
    onehot = (flat_ids[:, None] == jnp.arange(experts_all, dtype=jnp.int32)[None, :]).astype(
        jnp.int32
    )
    before = jnp.cumsum(onehot, axis=0) - onehot
    slot_index = jnp.sum(before * onehot, axis=1)
    target = (flat_ids * capacity + slot_index).reshape(rows_out, topk)
    matches = (
        target[:, :, None] == jnp.arange(experts_all * capacity, dtype=jnp.int32)[None, None, :]
    )
    placing = jnp.sum(matches.astype(jnp.int32), axis=1).astype(jnp.bfloat16)
    mixing = jnp.sum(
        jnp.where(matches, combine_weight.astype(jnp.float32)[:, :, None], 0.0), axis=1
    ).astype(jnp.bfloat16)
    outgoing = jnp.einsum("rs,rd->sd", placing, normed, preferred_element_type=jnp.float32).astype(
        jnp.bfloat16
    )
    outgoing = outgoing.reshape(experts_all, capacity, width)
    returned = lax.all_to_all(
        expert_block(
            lax.all_to_all(outgoing, ("head", "tok"), split_axis=0, concat_axis=0, tiled=True),
            w_gate_up[0],
            w_down[0],
        ),
        ("head", "tok"),
        split_axis=0,
        concat_axis=0,
        tiled=True,
    )
    back_rows = returned.reshape(experts_all * capacity, width)
    expert_sum = jnp.dot(mixing, back_rows, preferred_element_type=jnp.float32)
    return (hidden + expert_sum).astype(jnp.bfloat16)

def solution(mesh):
    placed = (
        P("tok", "head"),
        P(None, "tok", None),
        P(None, "tok", None),
        P(),
        P(),
        P("head", None),
        P(("tok", "head"), None),
        P(),
        P(("tok", "head"), None),
        P(("tok", "head"), None),
        P(),
        P(("head", "tok"), None, None),
        P(("head", "tok"), None, None),
    )
    return jax.shard_map(
        per_device, mesh=mesh, in_specs=placed, out_specs=P(("tok", "head"), None), check_vma=False
    )
```

```python
import functools

import jax
import jax.numpy as jnp
from jax import lax
from jax.experimental import pallas as pl
from jax.experimental.pallas import tpu as pltpu
from jax.sharding import PartitionSpec as P

HEADS = 64
KV_HEADS = 4
HD = 128


EPSILON = 1e-06


def rms_scale(values, gain):
    mean_square = jnp.mean(values * values, axis=-1, keepdims=True)
    return values * lax.rsqrt(mean_square + EPSILON) * gain


def expert_block(inputs, gate_up, down_proj):
    width = down_proj.shape[1]
    hidden_units = down_proj.shape[0]
    flat_rows = inputs.reshape(-1, width)
    both = jnp.dot(flat_rows, gate_up, preferred_element_type=jnp.float32)
    active = (jax.nn.silu(both[:, :hidden_units]) * both[:, hidden_units:]).astype(jnp.bfloat16)
    result = jnp.dot(active, down_proj, preferred_element_type=jnp.float32).astype(jnp.bfloat16)
    return result.reshape(inputs.shape)


DEPTH = 4
CORES = 2
CHUNKS = 8
GROUP = 4
FLIGHT = 2
VMEM_BYTES = 60 * 2**20
MESH = pl.DeviceIdType.MESH


def dot32(a, b):
    return jnp.dot(a, b, preferred_element_type=jnp.float32)


def layer_kernel(
    dims,
    queries_hbm,
    cache_hbm,
    new_kv_hbm,
    q_gain_ref,
    k_gain_ref,
    limit_ref,
    out_weight_hbm,
    residual_ref,
    gain_ref,
    ids_ref,
    combine_ref,
    gate_up_hbm,
    down_hbm,
    result_ref,
    queries,
    keyval,
    query_normed,
    mixed,
    weight_sum,
    attn,
    routing,
    select,
    spread,
    out_w,
    gate_up,
    down,
    part,
    part_y,
    sum_y,
    part_z,
    hidden,
    rows,
    acc,
    active,
    share,
    in_core,
    sum_core,
    in_ax,
    in_ay,
    sum_ax,
    sum_ay,
    in_bx,
    in_by,
    sum_b,
    in_z,
    load_sem,
    send_sem,
    recv_sem,
):
    nz, ny, nx, capacity = dims
    extra = 15 + nx
    head, tok = lax.axis_index("head"), lax.axis_index("tok")
    z, y = lax.div(head, ny), lax.rem(head, ny)
    x, core = lax.div(tok, CORES), lax.rem(tok, CORES)
    tok_count = nx * CORES
    width = hidden.shape[1]
    rows_out = hidden.shape[0]
    step = width // CHUNKS
    slots, tokens = select.shape
    topk = ids_ref.shape[0]
    hidden_units = down.shape[0]
    query_rows = queries.shape[0]
    local_heads = queries.shape[1] // HD
    cache_rows = cache_hbm.shape[1]
    segment = keyval.shape[1]
    columns = [pl.ds(k * step, step) for k in range(CHUNKS)]
    spans = columns[:-1] + [pl.ds(width - step, step + 128)]

    axes = {
        "z": (nz, z, lambda p: (p * ny + y, tok)),
        "y": (ny, y, lambda p: (z * ny + p, tok)),
        "x": (nx, x, lambda p: (head, p * CORES + core)),
        "core": (CORES, core, lambda p: (head, x * CORES + p)),
    }

    loads = []

    def load(src, dst):
        copy = pltpu.make_async_copy(src, dst, load_sem.at[len(loads)])
        copy.start()
        loads.append(copy)
        return copy

    kv_index = lax.div(head * local_heads, HEADS // KV_HEADS)
    kv_loads = [
        load(cache_hbm.at[kv_index], keyval.at[tok, pl.ds(0, cache_rows)]),
        load(new_kv_hbm.at[kv_index], keyval.at[tok, pl.ds(cache_rows, query_rows)]),
    ]
    query_load = load(queries_hbm, queries)
    out_w_loads = [load(out_weight_hbm.at[:, c], out_w.at[:, c]) for c in columns]
    gate_up_loads = [load(gate_up_hbm.at[0, c, :], gate_up.at[c, :]) for c in columns]
    down_loads = [load(down_hbm.at[0, :, c], down.at[:, c]) for c in columns]

    barrier = pltpu.get_barrier_semaphore()
    greeted = 0
    for n, me, device in axes.values():
        for i in range(1, n):
            pl.semaphore_signal(
                barrier, inc=1, device_id=device(lax.rem(me + i, n)), device_id_type=MESH
            )
            greeted += 1

    sends = []

    def send(stage, k, axis, source, target):
        n, me, device = axes[axis]
        for i in range(1, n):
            peer = lax.rem(me + i, n)
            copy = pltpu.make_async_remote_copy(
                src_ref=source(peer),
                dst_ref=target(i),
                send_sem=send_sem.at[stage, k, i - 1],
                recv_sem=recv_sem.at[stage, k, i - 1],
                device_id=device(peer),
                device_id_type=MESH,
            )
            copy.start()
            sends.append(copy)

    def spread_out(stage, k, axis, place):
        send(stage, k, axis, lambda _: place, lambda _: place)

    def arrive(stage, k, axis, region):
        n, me, device = axes[axis]
        for i in range(1, n):
            peer = lax.rem(me + n - i, n)
            place = region(i, peer)
            pltpu.make_async_remote_copy(
                src_ref=place,
                dst_ref=place,
                send_sem=send_sem.at[stage, k, i - 1],
                recv_sem=recv_sem.at[stage, k, i - 1],
                device_id=device(peer),
                device_id_type=MESH,
            ).wait_recv()

    def total(first, others):
        value = first.astype(jnp.float32)
        for other in others:
            value = value + other.astype(jnp.float32)
        return value

    def wavefront(stages):
        for turn in range(CHUNKS + stages[-1][0]):
            for offset, stage in reversed(stages):
                if 0 <= turn - offset < CHUNKS:
                    stage(turn - offset)

    lane = lax.broadcasted_iota(jnp.int32, (topk, 128), 1)
    turned = jnp.where(lane == lax.broadcasted_iota(jnp.int32, (topk, 128), 0), 1.0, 0.0)
    empty = lax.broadcasted_iota(jnp.int32, (rows_out, 128), 1) >= topk

    def by_row(ref):
        return lax.dot_general(
            ref[...].astype(jnp.float32),
            turned,
            (((0,), (0,)), ((), ())),
            preferred_element_type=jnp.float32,
        )

    routing[tok, z, y, :, :128] = jnp.where(empty, -1.0, by_row(ids_ref)).astype(jnp.bfloat16)
    routing[tok, z, y, :, 128:] = by_row(combine_ref).astype(jnp.bfloat16)
    for copy in kv_loads:
        copy.wait()
    keyval[tok, :, :HD] = rms_scale(
        keyval[tok, :, :HD].astype(jnp.float32), k_gain_ref[...]
    ).astype(jnp.bfloat16)
    pl.semaphore_wait(barrier, greeted)
    spread_out(0, 0, "x", keyval.at[tok])
    spread_out(1, 0, "core", keyval.at[tok])
    spread_out(2, 0, "z", routing.at[tok, z, y])
    query_load.wait()
    for j in range(local_heads):
        query_normed[j * query_rows : (j + 1) * query_rows] = rms_scale(
            queries[:, j * HD : (j + 1) * HD].astype(jnp.float32), q_gain_ref[...]
        ).astype(jnp.bfloat16)

    def attend(owner, first):
        key_at = lax.broadcasted_iota(jnp.int32, (query_rows, segment), 1)
        query_at = lax.broadcasted_iota(jnp.int32, (query_rows, segment), 0)
        seen = jnp.where(
            key_at < cache_rows,
            (owner * cache_rows + key_at < limit_ref[...]).astype(jnp.int32),
            (
                owner * query_rows + key_at - cache_rows <= tok * query_rows + query_at
            ).astype(jnp.int32),
        )

        for j in range(0, local_heads * query_rows, GROUP * query_rows):
            part_rows = pl.ds(j, GROUP * query_rows)
            scores = lax.dot_general(
                query_normed[part_rows],
                keyval[owner, :, :HD],
                (((1,), (1,)), ((), ())),
                preferred_element_type=jnp.float32,
            )
            scores = (scores * HD ** (-0.5)).reshape(GROUP, query_rows, segment)
            weights = jnp.where(seen[None] > 0, jnp.exp(scores), 0.0)
            weights = weights.reshape(GROUP * query_rows, segment)
            sums = weights[:, :128]
            for i in range(1, segment // 128):
                sums = sums + weights[:, i * 128 : (i + 1) * 128]
            value = dot32(weights.astype(jnp.bfloat16), keyval[owner, :, HD:])
            weight_sum[part_rows] = sums if first else weight_sum[part_rows] + sums
            mixed[part_rows] = value if first else mixed[part_rows] + value

    attend(tok, True)
    arrive(2, 0, "z", lambda i, p: routing.at[tok, p, y])
    spread_out(3, 0, "y", routing.at[tok, :, y])
    arrive(1, 0, "core", lambda i, p: keyval.at[x * CORES + p])
    attend(x * CORES + 1 - core, False)
    arrive(3, 0, "y", lambda i, p: routing.at[tok, :, p])
    spread_out(4, 0, "x", routing.at[tok])
    arrive(0, 0, "x", lambda i, p: keyval.at[p * CORES + core])
    for i in range(1, nx):
        spread_out(1, i, "core", keyval.at[lax.rem(x + nx - i, nx) * CORES + core])
    for i in range(1, nx):
        attend(lax.rem(x + nx - i, nx) * CORES + core, False)
    arrive(4, 0, "x", lambda i, p: routing.at[p * CORES + core])
    for q in range(nx):
        spread_out(5, q, "core", routing.at[q * CORES + core])
    for i in range(1, nx):
        near = lax.rem(x + nx - i, nx) * CORES
        arrive(1, i, "core", lambda _, p: keyval.at[near + p])
        attend(near + 1 - core, False)
    for j in range(local_heads):
        mine = pl.ds(j * query_rows, query_rows)
        attn[:, j * HD : (j + 1) * HD] = (
            mixed[mine] / jnp.sum(weight_sum[mine], axis=1, keepdims=True)
        ).astype(jnp.bfloat16)

    squares = []

    def project(k):
        c = columns[k]
        out_w_loads[k].wait()
        proj = dot32(attn[...], out_w[:, c]).astype(jnp.bfloat16)
        part[:, :, :, c] = proj.reshape(nz, ny, rows_out, step)
        send(6, k, "y", lambda p: part.at[:, p, :, c], lambda i: part_y.at[i - 1, :, :, c])
        if k == FLIGHT - 1:
            place_rows()

    def reduce_y(k):
        c = columns[k]
        arrive(6, k, "y", lambda i, p: part_y.at[i - 1, :, :, c])
        value = total(part[:, y, :, c], [part_y[i, :, :, c] for i in range(ny - 1)])
        sum_y[:, :, c] = value.astype(jnp.bfloat16)
        send(7, k, "z", lambda p: sum_y.at[p, :, c], lambda i: part_z.at[i - 1, :, c])

    def reduce_z(k):
        c = columns[k]
        arrive(7, k, "z", lambda i, p: part_z.at[i - 1, :, c])
        value = total(sum_y[z, :, c], [part_z[i, :, c] for i in range(nz - 1)])
        value = value + residual_ref[:, c].astype(jnp.float32)
        hidden[:, c] = value
        squares.append(jnp.sum(value * value, axis=1, keepdims=True))
        rows[tok, z, y, :, c] = (value * gain_ref[:, c]).astype(jnp.bfloat16)
        if k == CHUNKS - 1:
            scale = lax.rsqrt(sum(squares) / width + EPSILON)
            high = scale.astype(jnp.bfloat16).astype(jnp.float32)
            lane = lax.broadcasted_iota(jnp.int32, (rows_out, 128), 1)
            both = jnp.where(lane == 0, high, jnp.where(lane == 1, scale - high, 0.0))
            rows[tok, z, y, :, pl.ds(width, 128)] = both.astype(jnp.bfloat16)
        spread_out(8, k, "z", rows.at[tok, z, y, :, spans[k]])

    def far(i):
        return lax.rem(x + nx - i, nx) * CORES + core

    def gather_z(k):
        c = spans[k]
        arrive(8, k, "z", lambda i, p: rows.at[tok, p, y, :, c])
        spread_out(9, k, "yx"[k % 2], rows.at[tok, :, y, :, c])
        if k % 2:
            spread_out(10, k, "y", rows.at[tok, :, y, :, c])

    def gather_first(k):
        c = spans[k]
        if k % 2 == 0:
            arrive(9, k, "y", lambda i, p: rows.at[tok, :, p, :, c])
            spread_out(10, k, "x", rows.at[tok, :, :, :, c])
            spread_out(11, k, "core", rows.at[tok, :, :, :, c])
        else:
            arrive(9, k, "x", lambda i, p: rows.at[p * CORES + core, :, y, :, c])
            for i in range(1, nx):
                spread_out(extra + i, k, "y", rows.at[far(i), :, y, :, c])

    def gather_second(k):
        c = spans[k]
        if k % 2 == 0:
            arrive(10, k, "x", lambda i, p: rows.at[p * CORES + core, :, :, :, c])
        else:
            arrive(10, k, "y", lambda i, p: rows.at[tok, :, p, :, c])
            spread_out(11, k, "core", rows.at[tok, :, :, :, c])
            for i in range(1, nx):
                arrive(extra + i, k, "y", lambda _, p: rows.at[far(i), :, p, :, c])
        for i in range(1, nx):
            spread_out(11 + i, k, "core", rows.at[far(i), :, :, :, c])

    def up(k):
        c = spans[k]
        arrive(11, k, "core", lambda i, p: rows.at[x * CORES + p, :, :, :, c])
        for i in range(1, nx):
            near = lax.rem(x + nx - i, nx) * CORES
            arrive(11 + i, k, "core", lambda _, p: rows.at[near + p, :, :, :, c])
        picked = dot32(select[...], rows[:, :, :, :, c].reshape(tokens, -1))
        gate_up_loads[k].wait()
        both = dot32(picked[:, :step].astype(jnp.bfloat16), gate_up[columns[k], :])
        both = both if k == 0 else acc[...] + both
        if k == CHUNKS - 1:
            both = both * jnp.sum(picked[:, step:], axis=1, keepdims=True)
        acc[...] = both

    def place_rows():
        for q in range(nx):
            arrive(5, q, "core", lambda i, p: routing.at[q * CORES + p])
        own = (head * tok_count + tok).astype(jnp.float32)
        flat = routing[...].reshape(tokens, 256).astype(jnp.float32)
        named = flat[:, :128] == own
        chosen = jnp.sum(jnp.where(named, 1.0, 0.0), axis=1, keepdims=True)
        scale = jnp.sum(jnp.where(named, flat[:, 128:], 0.0), axis=1, keepdims=True)
        here = lax.broadcasted_iota(jnp.int32, (tokens, tokens), 0)
        there = lax.broadcasted_iota(jnp.int32, (tokens, tokens), 1)
        earlier = (there < here) & (there >= here - lax.rem(here, rows_out))
        before = dot32(
            jnp.where(earlier, 1.0, 0.0).astype(jnp.bfloat16),
            jnp.broadcast_to(chosen, (tokens, 128)).astype(jnp.bfloat16),
        )[:, :1]
        at = lax.broadcasted_iota(jnp.int32, (tokens, 1), 0)
        start = lax.div(at, rows_out) * capacity
        place = jnp.where(chosen > 0.0, start.astype(jnp.float32) + before, -1.0)
        slot = lax.broadcasted_iota(jnp.int32, (tokens, slots), 1)
        hit = slot == place.astype(jnp.int32)
        spread[...] = jnp.where(hit, scale, 0.0).astype(jnp.bfloat16)
        select[...] = jnp.where(hit, 1.0, 0.0).T.astype(jnp.bfloat16)

    wavefront(
        [
            (0, project),
            (FLIGHT, reduce_y),
            (2 * FLIGHT, reduce_z),
            (3 * FLIGHT, gather_z),
            (4 * FLIGHT + 1, gather_first),
            (5 * FLIGHT + 2, gather_second),
            (6 * FLIGHT + 2, up),
        ]
    )

    gate = acc[:, :hidden_units]
    active[...] = (jax.nn.silu(gate) * acc[:, hidden_units:]).astype(jnp.bfloat16)

    base = 11 + nx

    def give(k):
        c = columns[k]
        down_loads[k].wait()
        expert_out = dot32(active[...], down[:, c]).astype(jnp.bfloat16)
        weighted = dot32(spread[...], expert_out).astype(jnp.bfloat16)
        share[:, :, :, :, :, c] = weighted.reshape(nx, CORES, nz, ny, rows_out, step)
        send(
            base,
            k,
            "core",
            lambda p: share.at[:, p, :, :, :, c],
            lambda i: in_core.at[:, :, :, :, c],
        )

    def return_core(k):
        c = columns[k]
        arrive(base, k, "core", lambda i, p: in_core.at[:, :, :, :, c])
        value = total(share[:, core, :, :, :, c], [in_core[:, :, :, :, c]])
        sum_core[:, :, :, :, c] = value.astype(jnp.bfloat16)
        if k % 2 == 0:
            send(
                base + 1,
                k,
                "x",
                lambda p: sum_core.at[p, :, :, :, c],
                lambda i: in_ax.at[i - 1, :, :, :, c],
            )
        else:
            send(
                base + 1,
                k,
                "y",
                lambda p: sum_core.at[:, :, p, :, c],
                lambda i: in_ay.at[i - 1, :, :, :, c],
            )

    def return_first(k):
        c = columns[k]
        if k % 2 == 0:
            arrive(base + 1, k, "x", lambda i, p: in_ax.at[i - 1, :, :, :, c])
            value = total(
                sum_core[x, :, :, :, c], [in_ax[i, :, :, :, c] for i in range(nx - 1)]
            )
            sum_ax[:, :, :, c] = value.astype(jnp.bfloat16)
            send(
                base + 2,
                k,
                "y",
                lambda p: sum_ax.at[:, p, :, c],
                lambda i: in_by.at[i - 1, :, :, c],
            )
        else:
            arrive(base + 1, k, "y", lambda i, p: in_ay.at[i - 1, :, :, :, c])
            value = total(
                sum_core[:, :, y, :, c], [in_ay[i, :, :, :, c] for i in range(ny - 1)]
            )
            sum_ay[:, :, :, c] = value.astype(jnp.bfloat16)
            send(
                base + 2,
                k,
                "x",
                lambda p: sum_ay.at[p, :, :, c],
                lambda i: in_bx.at[i - 1, :, :, c],
            )

    def return_second(k):
        c = columns[k]
        if k % 2 == 0:
            arrive(base + 2, k, "y", lambda i, p: in_by.at[i - 1, :, :, c])
            value = total(sum_ax[:, y, :, c], [in_by[i, :, :, c] for i in range(ny - 1)])
        else:
            arrive(base + 2, k, "x", lambda i, p: in_bx.at[i - 1, :, :, c])
            value = total(sum_ay[x, :, :, c], [in_bx[i, :, :, c] for i in range(nx - 1)])
        sum_b[:, :, c] = value.astype(jnp.bfloat16)
        send(base + 3, k, "z", lambda p: sum_b.at[p, :, c], lambda i: in_z.at[i - 1, :, c])

    def return_z(k):
        c = columns[k]
        arrive(base + 3, k, "z", lambda i, p: in_z.at[i - 1, :, c])
        value = total(sum_b[z, :, c], [in_z[i, :, c] for i in range(nz - 1)])
        result_ref[:, c] = (hidden[:, c] + value).astype(jnp.bfloat16)

    wavefront(
        [
            (0, give),
            (FLIGHT, return_core),
            (2 * FLIGHT + 1, return_first),
            (3 * FLIGHT + 2, return_second),
            (4 * FLIGHT + 2, return_z),
        ]
    )
    for copy in sends:
        copy.wait_send()


def routed_layer(
    queries,
    cache,
    new_kv,
    q_gain,
    k_gain,
    out_weight,
    residual,
    norm_gain,
    expert_ids,
    combine_weight,
    prefix_len,
    w_gate_up,
    w_down,
):
    head_count = lax.axis_size("head")
    tok_count = lax.axis_size("tok")
    nz, ny, nx = DEPTH, head_count // DEPTH, tok_count // CORES
    width = out_weight.shape[1]
    rows_out, topk = expert_ids.shape
    experts_all = head_count * tok_count
    tokens = rows_out * experts_all
    capacity = max(2, 2 * rows_out * topk // experts_all)
    slots = experts_all * capacity
    hidden_units = w_down.shape[1]

    b16, f32 = jnp.bfloat16, jnp.float32
    vmem = pl.BlockSpec(memory_space=pltpu.VMEM)
    hbm = pl.BlockSpec(memory_space=pl.ANY)
    stages = 15 + 2 * nx
    query_rows = queries.shape[0]
    heads = queries.shape[1] // HD
    segment = cache.shape[1] + query_rows
    widest = max(nz, ny, nx, CORES) - 1
    scratch = [
        pltpu.VMEM(queries.shape, b16),
        pltpu.VMEM((tok_count, segment, 2 * HD), b16),
        pltpu.VMEM((heads * query_rows, HD), b16),
        pltpu.VMEM((heads * query_rows, HD), f32),
        pltpu.VMEM((heads * query_rows, 128), f32),
        pltpu.VMEM(queries.shape, b16),
        pltpu.VMEM((tok_count, nz, ny, rows_out, 256), b16),
        pltpu.VMEM((slots, tokens), b16),
        pltpu.VMEM((tokens, slots), b16),
        pltpu.VMEM(out_weight.shape, b16),
        pltpu.VMEM(w_gate_up.shape[1:], b16),
        pltpu.VMEM(w_down.shape[1:], b16),
        pltpu.VMEM((nz, ny, rows_out, width), b16),
        pltpu.VMEM((ny - 1, nz, rows_out, width), b16),
        pltpu.VMEM((nz, rows_out, width), b16),
        pltpu.VMEM((nz - 1, rows_out, width), b16),
        pltpu.VMEM((rows_out, width), f32),
        pltpu.VMEM((tok_count, nz, ny, rows_out, width + 128), b16),
        pltpu.VMEM((slots, 2 * hidden_units), f32),
        pltpu.VMEM((slots, hidden_units), b16),
        pltpu.VMEM((nx, CORES, nz, ny, rows_out, width), b16),
        pltpu.VMEM((nx, nz, ny, rows_out, width), b16),
        pltpu.VMEM((nx, nz, ny, rows_out, width), b16),
        pltpu.VMEM((nx - 1, nz, ny, rows_out, width), b16),
        pltpu.VMEM((ny - 1, nx, nz, rows_out, width), b16),
        pltpu.VMEM((nz, ny, rows_out, width), b16),
        pltpu.VMEM((nx, nz, rows_out, width), b16),
        pltpu.VMEM((nx - 1, nz, rows_out, width), b16),
        pltpu.VMEM((ny - 1, nz, rows_out, width), b16),
        pltpu.VMEM((nz, rows_out, width), b16),
        pltpu.VMEM((nz - 1, rows_out, width), b16),
        pltpu.SemaphoreType.DMA((3 + 3 * CHUNKS,)),
        pltpu.SemaphoreType.DMA((stages, CHUNKS, widest)),
        pltpu.SemaphoreType.DMA((stages, CHUNKS, widest)),
    ]
    return pl.pallas_call(
        functools.partial(layer_kernel, (nz, ny, nx, capacity)),
        out_shape=jax.ShapeDtypeStruct((rows_out, width), b16),
        in_specs=[hbm] * 3 + [vmem] * 3 + [hbm] + [vmem] * 4 + [hbm] * 2,
        out_specs=vmem,
        scratch_shapes=scratch,
        compiler_params=pltpu.CompilerParams(
            collective_id=0, has_side_effects=True, vmem_limit_bytes=VMEM_BYTES
        ),
    )(
        queries,
        cache,
        new_kv,
        q_gain.reshape(1, HD),
        k_gain.reshape(1, HD),
        prefix_len.reshape(1, 1),
        out_weight,
        residual,
        norm_gain.reshape(1, width),
        expert_ids.T,
        combine_weight.T,
        w_gate_up,
        w_down,
    )


def fits(tokens, width, experts, spans, heads):
    if spans > CORES * CHUNKS or heads % GROUP:
        return False
    return 12 * tokens * width <= VMEM_BYTES // 2 and experts <= 256


def per_device(
    queries,
    cache,
    new_kv,
    q_gain,
    k_gain,
    out_weight,
    residual,
    norm_gain,
    expert_ids,
    combine_weight,
    prefix_len,
    w_gate_up,
    w_down,
):
    head_count = lax.axis_size("head")
    tok_count = lax.axis_size("tok")
    query_rows = queries.shape[0]
    local_heads = queries.shape[1] // HD
    experts_all = head_count * tok_count
    tokens = query_rows * tok_count
    if fits(tokens, out_weight.shape[1], experts_all, tok_count, local_heads):
        return routed_layer(
            queries,
            cache,
            new_kv,
            q_gain,
            k_gain,
            out_weight,
            residual,
            norm_gain,
            expert_ids,
            combine_weight,
            prefix_len,
            w_gate_up,
            w_down,
        )
    cache_rows = cache.shape[1]
    segment = cache_rows + query_rows
    kv_index = lax.axis_index("head") * local_heads // (HEADS // KV_HEADS)
    query_normed = rms_scale(
        queries.reshape(query_rows, local_heads, HD).astype(jnp.float32), q_gain
    ).astype(jnp.bfloat16)
    own_block = jnp.concatenate(
        [
            lax.dynamic_index_in_dim(cache, kv_index, 0, keepdims=False),
            lax.dynamic_index_in_dim(new_kv, kv_index, 0, keepdims=False),
        ],
        axis=0,
    )
    key_part = rms_scale(own_block[:, :HD].astype(jnp.float32), k_gain).astype(jnp.bfloat16)
    key_block = jnp.concatenate([key_part, own_block[:, HD:]], axis=1)
    query_position = lax.axis_index("tok") * query_rows + jnp.arange(query_rows, dtype=jnp.int32)
    limit = prefix_len[0]
    piece = lax.all_gather(key_block, "tok", axis=0, tiled=True)
    position = jnp.arange(piece.shape[0], dtype=jnp.int32)
    shard = position // segment
    offset = position % segment
    in_cache = offset < cache_rows
    cache_position = shard * cache_rows + offset
    span_position = shard * query_rows + offset - cache_rows
    visible = jnp.where(
        in_cache[None, :],
        (cache_position < limit)[None, :],
        span_position[None, :] <= query_position[:, None],
    )
    scores = jnp.einsum(
        "qhd,kd->qhk", query_normed, piece[:, :HD], preferred_element_type=jnp.float32
    ) * HD ** (-0.5)
    weights = jnp.where(visible[:, None, :], jnp.exp(scores), 0.0)
    accum = jnp.einsum(
        "qhk,kd->qhd",
        weights.astype(jnp.bfloat16),
        piece[:, HD:],
        preferred_element_type=jnp.float32,
    )
    total = jnp.sum(weights, axis=2)
    accum, total = (accum, total)
    attn = (accum / total[:, :, None]).astype(jnp.bfloat16).reshape(query_rows, local_heads * HD)
    rows_out = query_rows // head_count
    full_proj = lax.psum(
        jnp.dot(attn, out_weight, preferred_element_type=jnp.float32).astype(jnp.bfloat16), "head"
    ).astype(jnp.float32)
    attn_proj = lax.dynamic_slice_in_dim(full_proj, lax.axis_index("head") * rows_out, rows_out, 0)
    hidden = residual.astype(jnp.float32) + attn_proj
    normed = rms_scale(hidden, norm_gain).astype(jnp.bfloat16)
    width = normed.shape[1]
    experts_all = head_count * tok_count
    topk = expert_ids.shape[1]
    capacity = max(2, 2 * rows_out * topk // experts_all)
    flat_ids = expert_ids.reshape(-1)
    onehot = (flat_ids[:, None] == jnp.arange(experts_all, dtype=jnp.int32)[None, :]).astype(
        jnp.int32
    )
    before = jnp.cumsum(onehot, axis=0) - onehot
    slot_index = jnp.sum(before * onehot, axis=1)
    target = (flat_ids * capacity + slot_index).reshape(rows_out, topk)
    matches = (
        target[:, :, None] == jnp.arange(experts_all * capacity, dtype=jnp.int32)[None, None, :]
    )
    placing = jnp.sum(matches.astype(jnp.int32), axis=1).astype(jnp.bfloat16)
    mixing = jnp.sum(
        jnp.where(matches, combine_weight.astype(jnp.float32)[:, :, None], 0.0), axis=1
    ).astype(jnp.bfloat16)
    outgoing = jnp.einsum("rs,rd->sd", placing, normed, preferred_element_type=jnp.float32).astype(
        jnp.bfloat16
    )
    outgoing = outgoing.reshape(experts_all, capacity, width)
    returned = lax.all_to_all(
        expert_block(
            lax.all_to_all(outgoing, ("head", "tok"), split_axis=0, concat_axis=0, tiled=True),
            w_gate_up[0],
            w_down[0],
        ),
        ("head", "tok"),
        split_axis=0,
        concat_axis=0,
        tiled=True,
    )
    back_rows = returned.reshape(experts_all * capacity, width)
    expert_sum = jnp.dot(mixing, back_rows, preferred_element_type=jnp.float32)
    return (hidden + expert_sum).astype(jnp.bfloat16)

def solution(mesh):
    placed = (
        P("tok", "head"),
        P(None, "tok", None),
        P(None, "tok", None),
        P(),
        P(),
        P("head", None),
        P(("tok", "head"), None),
        P(),
        P(("tok", "head"), None),
        P(("tok", "head"), None),
        P(),
        P(("head", "tok"), None, None),
        P(("head", "tok"), None, None),
    )
    return jax.shard_map(
        per_device, mesh=mesh, in_specs=placed, out_specs=P(("tok", "head"), None), check_vma=False
    )
```

```python
import functools

import jax
import jax.numpy as jnp
from jax import lax
from jax.experimental import pallas as pl
from jax.experimental.pallas import tpu as pltpu
from jax.sharding import PartitionSpec as P

HEADS = 64
KV_HEADS = 4
HD = 128


EPSILON = 1e-06


def rms_scale(values, gain):
    mean_square = jnp.mean(values * values, axis=-1, keepdims=True)
    return values * lax.rsqrt(mean_square + EPSILON) * gain


def expert_block(inputs, gate_up, down_proj):
    width = down_proj.shape[1]
    hidden_units = down_proj.shape[0]
    flat_rows = inputs.reshape(-1, width)
    both = jnp.dot(flat_rows, gate_up, preferred_element_type=jnp.float32)
    active = (jax.nn.silu(both[:, :hidden_units]) * both[:, hidden_units:]).astype(jnp.bfloat16)
    result = jnp.dot(active, down_proj, preferred_element_type=jnp.float32).astype(jnp.bfloat16)
    return result.reshape(inputs.shape)


DEPTH = 4
CORES = 2
CHUNKS = 8
GROUP = 4
FLIGHT = 2
VMEM_BYTES = 60 * 2**20
MESH = pl.DeviceIdType.MESH


def dot32(a, b):
    return jnp.dot(a, b, preferred_element_type=jnp.float32)


def layer_kernel(
    dims,
    queries_hbm,
    cache_hbm,
    new_kv_hbm,
    q_gain_ref,
    k_gain_ref,
    limit_ref,
    out_weight_hbm,
    residual_ref,
    gain_ref,
    ids_ref,
    combine_ref,
    gate_up_hbm,
    down_hbm,
    result_ref,
    queries,
    keyval,
    query_normed,
    mixed,
    weight_sum,
    attn,
    routing,
    select,
    spread,
    out_w,
    gate_up,
    down,
    part,
    part_y,
    sum_y,
    part_v,
    sum_v,
    part_z,
    hidden,
    rows,
    acc,
    active,
    share,
    in_core,
    sum_core,
    in_ax,
    in_ay,
    sum_ax,
    sum_ay,
    in_bx,
    in_by,
    sum_b,
    in_v,
    sum_w,
    in_z,
    load_sem,
    send_sem,
    recv_sem,
):
    nz, ny, nx, capacity = dims
    extra = 15 + nx
    more = 15 + 2 * nx
    head, tok = lax.axis_index("head"), lax.axis_index("tok")
    z, y = lax.div(head, ny), lax.rem(head, ny)
    zh, zl = lax.div(z, 2), lax.rem(z, 2)
    x, core = lax.div(tok, CORES), lax.rem(tok, CORES)
    tok_count = nx * CORES
    width = hidden.shape[1]
    rows_out = hidden.shape[0]
    step = width // CHUNKS
    slots, tokens = select.shape
    topk = ids_ref.shape[0]
    hidden_units = down.shape[0]
    query_rows = queries.shape[0]
    local_heads = queries.shape[1] // HD
    cache_rows = cache_hbm.shape[1]
    segment = keyval.shape[1]
    columns = [pl.ds(k * step, step) for k in range(CHUNKS)]
    spans = columns[:-1] + [pl.ds(width - step, step + 128)]

    axes = {
        "far_z": (nz // 2, zh, lambda p: ((p * 2 + zl) * ny + y, tok)),
        "near_z": (2, zl, lambda p: ((zh * 2 + p) * ny + y, tok)),
        "y": (ny, y, lambda p: (z * ny + p, tok)),
        "x": (nx, x, lambda p: (head, p * CORES + core)),
        "core": (CORES, core, lambda p: (head, x * CORES + p)),
    }

    loads = []

    def load(src, dst):
        copy = pltpu.make_async_copy(src, dst, load_sem.at[len(loads)])
        copy.start()
        loads.append(copy)
        return copy

    kv_index = lax.div(head * local_heads, HEADS // KV_HEADS)
    kv_loads = [
        load(cache_hbm.at[kv_index], keyval.at[tok, pl.ds(0, cache_rows)]),
        load(new_kv_hbm.at[kv_index], keyval.at[tok, pl.ds(cache_rows, query_rows)]),
    ]
    query_load = load(queries_hbm, queries)
    out_w_loads = [load(out_weight_hbm.at[:, c], out_w.at[:, c]) for c in columns]
    gate_up_loads = [load(gate_up_hbm.at[0, c, :], gate_up.at[c, :]) for c in columns]
    down_loads = [load(down_hbm.at[0, :, c], down.at[:, c]) for c in columns]

    barrier = pltpu.get_barrier_semaphore()
    greeted = 0
    for n, me, device in axes.values():
        for i in range(1, n):
            pl.semaphore_signal(
                barrier, inc=1, device_id=device(lax.rem(me + i, n)), device_id_type=MESH
            )
            greeted += 1

    sends = []

    def send(stage, k, axis, source, target):
        n, me, device = axes[axis]
        for i in range(1, n):
            peer = lax.rem(me + i, n)
            copy = pltpu.make_async_remote_copy(
                src_ref=source(peer),
                dst_ref=target(i),
                send_sem=send_sem.at[stage, k, i - 1],
                recv_sem=recv_sem.at[stage, k, i - 1],
                device_id=device(peer),
                device_id_type=MESH,
            )
            copy.start()
            sends.append(copy)

    def spread_out(stage, k, axis, place):
        send(stage, k, axis, lambda _: place, lambda _: place)

    def arrive(stage, k, axis, region):
        n, me, device = axes[axis]
        for i in range(1, n):
            peer = lax.rem(me + n - i, n)
            place = region(i, peer)
            pltpu.make_async_remote_copy(
                src_ref=place,
                dst_ref=place,
                send_sem=send_sem.at[stage, k, i - 1],
                recv_sem=recv_sem.at[stage, k, i - 1],
                device_id=device(peer),
                device_id_type=MESH,
            ).wait_recv()

    def total(first, others):
        value = first.astype(jnp.float32)
        for other in others:
            value = value + other.astype(jnp.float32)
        return value

    def wavefront(stages):
        for turn in range(CHUNKS + stages[-1][0]):
            for offset, stage in reversed(stages):
                if 0 <= turn - offset < CHUNKS:
                    stage(turn - offset)

    lane = lax.broadcasted_iota(jnp.int32, (topk, 128), 1)
    turned = jnp.where(lane == lax.broadcasted_iota(jnp.int32, (topk, 128), 0), 1.0, 0.0)
    empty = lax.broadcasted_iota(jnp.int32, (rows_out, 128), 1) >= topk

    def by_row(ref):
        return lax.dot_general(
            ref[...].astype(jnp.float32),
            turned,
            (((0,), (0,)), ((), ())),
            preferred_element_type=jnp.float32,
        )

    routing[tok, zh, zl, y, :, :128] = jnp.where(empty, -1.0, by_row(ids_ref)).astype(jnp.bfloat16)
    routing[tok, zh, zl, y, :, 128:] = by_row(combine_ref).astype(jnp.bfloat16)
    for copy in kv_loads:
        copy.wait()
    keyval[tok, :, :HD] = rms_scale(
        keyval[tok, :, :HD].astype(jnp.float32), k_gain_ref[...]
    ).astype(jnp.bfloat16)
    pl.semaphore_wait(barrier, greeted)
    spread_out(0, 0, "x", keyval.at[tok])
    spread_out(1, 0, "core", keyval.at[tok])
    spread_out(2, 0, "far_z", routing.at[tok, zh, zl, y])
    query_load.wait()
    for j in range(local_heads):
        query_normed[j * query_rows : (j + 1) * query_rows] = rms_scale(
            queries[:, j * HD : (j + 1) * HD].astype(jnp.float32), q_gain_ref[...]
        ).astype(jnp.bfloat16)

    def attend(owner, first):
        key_at = lax.broadcasted_iota(jnp.int32, (query_rows, segment), 1)
        query_at = lax.broadcasted_iota(jnp.int32, (query_rows, segment), 0)
        seen = jnp.where(
            key_at < cache_rows,
            (owner * cache_rows + key_at < limit_ref[...]).astype(jnp.int32),
            (
                owner * query_rows + key_at - cache_rows <= tok * query_rows + query_at
            ).astype(jnp.int32),
        )

        for j in range(0, local_heads * query_rows, GROUP * query_rows):
            part_rows = pl.ds(j, GROUP * query_rows)
            scores = lax.dot_general(
                query_normed[part_rows],
                keyval[owner, :, :HD],
                (((1,), (1,)), ((), ())),
                preferred_element_type=jnp.float32,
            )
            scores = (scores * HD ** (-0.5)).reshape(GROUP, query_rows, segment)
            weights = jnp.where(seen[None] > 0, jnp.exp(scores), 0.0)
            weights = weights.reshape(GROUP * query_rows, segment)
            sums = weights[:, :128]
            for i in range(1, segment // 128):
                sums = sums + weights[:, i * 128 : (i + 1) * 128]
            value = dot32(weights.astype(jnp.bfloat16), keyval[owner, :, HD:])
            weight_sum[part_rows] = sums if first else weight_sum[part_rows] + sums
            mixed[part_rows] = value if first else mixed[part_rows] + value

    attend(tok, True)
    arrive(2, 0, "far_z", lambda i, p: routing.at[tok, p, zl, y])
    spread_out(more, 0, "near_z", routing.at[tok, :, zl, y])
    arrive(1, 0, "core", lambda i, p: keyval.at[x * CORES + p])
    arrive(more, 0, "near_z", lambda i, p: routing.at[tok, :, p, y])
    spread_out(3, 0, "y", routing.at[tok, :, :, y])
    attend(x * CORES + 1 - core, False)
    arrive(3, 0, "y", lambda i, p: routing.at[tok, :, :, p])
    spread_out(4, 0, "x", routing.at[tok])
    arrive(0, 0, "x", lambda i, p: keyval.at[p * CORES + core])
    for i in range(1, nx):
        spread_out(1, i, "core", keyval.at[lax.rem(x + nx - i, nx) * CORES + core])
    for i in range(1, nx):
        attend(lax.rem(x + nx - i, nx) * CORES + core, False)
    arrive(4, 0, "x", lambda i, p: routing.at[p * CORES + core])
    for q in range(nx):
        spread_out(5, q, "core", routing.at[q * CORES + core])
    for i in range(1, nx):
        near = lax.rem(x + nx - i, nx) * CORES
        arrive(1, i, "core", lambda _, p: keyval.at[near + p])
        attend(near + 1 - core, False)
    for j in range(local_heads):
        mine = pl.ds(j * query_rows, query_rows)
        attn[:, j * HD : (j + 1) * HD] = (
            mixed[mine] / jnp.sum(weight_sum[mine], axis=1, keepdims=True)
        ).astype(jnp.bfloat16)

    squares = []

    def project(k):
        c = columns[k]
        out_w_loads[k].wait()
        proj = dot32(attn[...], out_w[:, c]).astype(jnp.bfloat16)
        part[:, :, :, c] = proj.reshape(nz, ny, rows_out, step)
        send(6, k, "y", lambda p: part.at[:, p, :, c], lambda i: part_y.at[i - 1, :, :, c])
        if k == FLIGHT - 1:
            place_rows()

    def reduce_y(k):
        c = columns[k]
        arrive(6, k, "y", lambda i, p: part_y.at[i - 1, :, :, c])
        value = total(part[:, y, :, c], [part_y[i, :, :, c] for i in range(ny - 1)])
        sum_y[:, :, :, c] = value.reshape(nz // 2, 2, rows_out, step).astype(jnp.bfloat16)
        send(
            7, k, "near_z", lambda p: sum_y.at[:, p, :, c], lambda i: part_v.at[i - 1, :, :, c]
        )

    def reduce_near(k):
        c = columns[k]
        arrive(7, k, "near_z", lambda i, p: part_v.at[i - 1, :, :, c])
        value = total(sum_y[:, zl, :, c], [part_v[0, :, :, c]])
        sum_v[:, :, c] = value.astype(jnp.bfloat16)
        send(
            more + 1, k, "far_z", lambda p: sum_v.at[p, :, c], lambda i: part_z.at[i - 1, :, c]
        )

    def reduce_z(k):
        c = columns[k]
        arrive(more + 1, k, "far_z", lambda i, p: part_z.at[i - 1, :, c])
        value = total(sum_v[zh, :, c], [part_z[i, :, c] for i in range(nz // 2 - 1)])
        value = value + residual_ref[:, c].astype(jnp.float32)
        hidden[:, c] = value
        squares.append(jnp.sum(value * value, axis=1, keepdims=True))
        rows[tok, zh, zl, y, :, c] = (value * gain_ref[:, c]).astype(jnp.bfloat16)
        if k == CHUNKS - 1:
            scale = lax.rsqrt(sum(squares) / width + EPSILON)
            high = scale.astype(jnp.bfloat16).astype(jnp.float32)
            lane = lax.broadcasted_iota(jnp.int32, (rows_out, 128), 1)
            both = jnp.where(lane == 0, high, jnp.where(lane == 1, scale - high, 0.0))
            rows[tok, zh, zl, y, :, pl.ds(width, 128)] = both.astype(jnp.bfloat16)
        spread_out(8, k, "far_z", rows.at[tok, zh, zl, y, :, spans[k]])

    def far(i):
        return lax.rem(x + nx - i, nx) * CORES + core

    def gather_far(k):
        c = spans[k]
        arrive(8, k, "far_z", lambda i, p: rows.at[tok, p, zl, y, :, c])
        spread_out(more + 2, k, "near_z", rows.at[tok, :, zl, y, :, c])

    def gather_z(k):
        c = spans[k]
        arrive(more + 2, k, "near_z", lambda i, p: rows.at[tok, :, p, y, :, c])
        spread_out(9, k, "yx"[k % 2], rows.at[tok, :, :, y, :, c])
        if k % 2:
            spread_out(10, k, "y", rows.at[tok, :, :, y, :, c])

    def gather_first(k):
        c = spans[k]
        if k % 2 == 0:
            arrive(9, k, "y", lambda i, p: rows.at[tok, :, :, p, :, c])
            spread_out(10, k, "x", rows.at[tok, :, :, :, :, c])
            spread_out(11, k, "core", rows.at[tok, :, :, :, :, c])
        else:
            arrive(9, k, "x", lambda i, p: rows.at[p * CORES + core, :, :, y, :, c])
            for i in range(1, nx):
                spread_out(extra + i, k, "y", rows.at[far(i), :, :, y, :, c])

    def gather_second(k):
        c = spans[k]
        if k % 2 == 0:
            arrive(10, k, "x", lambda i, p: rows.at[p * CORES + core, :, :, :, :, c])
        else:
            arrive(10, k, "y", lambda i, p: rows.at[tok, :, :, p, :, c])
            spread_out(11, k, "core", rows.at[tok, :, :, :, :, c])
            for i in range(1, nx):
                arrive(extra + i, k, "y", lambda _, p: rows.at[far(i), :, :, p, :, c])
        for i in range(1, nx):
            spread_out(11 + i, k, "core", rows.at[far(i), :, :, :, :, c])

    def up(k):
        c = spans[k]
        arrive(11, k, "core", lambda i, p: rows.at[x * CORES + p, :, :, :, :, c])
        for i in range(1, nx):
            near = lax.rem(x + nx - i, nx) * CORES
            arrive(11 + i, k, "core", lambda _, p: rows.at[near + p, :, :, :, :, c])
        picked = dot32(select[...], rows[:, :, :, :, :, c].reshape(tokens, -1))
        gate_up_loads[k].wait()
        both = dot32(picked[:, :step].astype(jnp.bfloat16), gate_up[columns[k], :])
        both = both if k == 0 else acc[...] + both
        if k == CHUNKS - 1:
            both = both * jnp.sum(picked[:, step:], axis=1, keepdims=True)
        acc[...] = both

    def place_rows():
        for q in range(nx):
            arrive(5, q, "core", lambda i, p: routing.at[q * CORES + p])
        own = (head * tok_count + tok).astype(jnp.float32)
        flat = routing[...].reshape(tokens, 256).astype(jnp.float32)
        named = flat[:, :128] == own
        chosen = jnp.sum(jnp.where(named, 1.0, 0.0), axis=1, keepdims=True)
        scale = jnp.sum(jnp.where(named, flat[:, 128:], 0.0), axis=1, keepdims=True)
        here = lax.broadcasted_iota(jnp.int32, (tokens, tokens), 0)
        there = lax.broadcasted_iota(jnp.int32, (tokens, tokens), 1)
        earlier = (there < here) & (there >= here - lax.rem(here, rows_out))
        before = dot32(
            jnp.where(earlier, 1.0, 0.0).astype(jnp.bfloat16),
            jnp.broadcast_to(chosen, (tokens, 128)).astype(jnp.bfloat16),
        )[:, :1]
        at = lax.broadcasted_iota(jnp.int32, (tokens, 1), 0)
        start = lax.div(at, rows_out) * capacity
        place = jnp.where(chosen > 0.0, start.astype(jnp.float32) + before, -1.0)
        slot = lax.broadcasted_iota(jnp.int32, (tokens, slots), 1)
        hit = slot == place.astype(jnp.int32)
        spread[...] = jnp.where(hit, scale, 0.0).astype(jnp.bfloat16)
        select[...] = jnp.where(hit, 1.0, 0.0).T.astype(jnp.bfloat16)

    wavefront(
        [
            (0, project),
            (FLIGHT, reduce_y),
            (2 * FLIGHT, reduce_near),
            (3 * FLIGHT, reduce_z),
            (4 * FLIGHT, gather_far),
            (5 * FLIGHT, gather_z),
            (6 * FLIGHT + 1, gather_first),
            (7 * FLIGHT + 2, gather_second),
            (8 * FLIGHT + 2, up),
        ]
    )

    gate = acc[:, :hidden_units]
    active[...] = (jax.nn.silu(gate) * acc[:, hidden_units:]).astype(jnp.bfloat16)

    base = 11 + nx

    def give(k):
        c = columns[k]
        down_loads[k].wait()
        expert_out = dot32(active[...], down[:, c]).astype(jnp.bfloat16)
        weighted = dot32(spread[...], expert_out).astype(jnp.bfloat16)
        share[:, :, :, :, :, c] = weighted.reshape(nx, CORES, nz, ny, rows_out, step)
        send(
            base,
            k,
            "core",
            lambda p: share.at[:, p, :, :, :, c],
            lambda i: in_core.at[:, :, :, :, c],
        )

    def return_core(k):
        c = columns[k]
        arrive(base, k, "core", lambda i, p: in_core.at[:, :, :, :, c])
        value = total(share[:, core, :, :, :, c], [in_core[:, :, :, :, c]])
        sum_core[:, :, :, :, c] = value.astype(jnp.bfloat16)
        if k % 2 == 0:
            send(
                base + 1,
                k,
                "x",
                lambda p: sum_core.at[p, :, :, :, c],
                lambda i: in_ax.at[i - 1, :, :, :, c],
            )
        else:
            send(
                base + 1,
                k,
                "y",
                lambda p: sum_core.at[:, :, p, :, c],
                lambda i: in_ay.at[i - 1, :, :, :, c],
            )

    def return_first(k):
        c = columns[k]
        if k % 2 == 0:
            arrive(base + 1, k, "x", lambda i, p: in_ax.at[i - 1, :, :, :, c])
            value = total(
                sum_core[x, :, :, :, c], [in_ax[i, :, :, :, c] for i in range(nx - 1)]
            )
            sum_ax[:, :, :, c] = value.astype(jnp.bfloat16)
            send(
                base + 2,
                k,
                "y",
                lambda p: sum_ax.at[:, p, :, c],
                lambda i: in_by.at[i - 1, :, :, c],
            )
        else:
            arrive(base + 1, k, "y", lambda i, p: in_ay.at[i - 1, :, :, :, c])
            value = total(
                sum_core[:, :, y, :, c], [in_ay[i, :, :, :, c] for i in range(ny - 1)]
            )
            sum_ay[:, :, :, c] = value.astype(jnp.bfloat16)
            send(
                base + 2,
                k,
                "x",
                lambda p: sum_ay.at[p, :, :, c],
                lambda i: in_bx.at[i - 1, :, :, c],
            )

    def return_second(k):
        c = columns[k]
        if k % 2 == 0:
            arrive(base + 2, k, "y", lambda i, p: in_by.at[i - 1, :, :, c])
            value = total(sum_ax[:, y, :, c], [in_by[i, :, :, c] for i in range(ny - 1)])
        else:
            arrive(base + 2, k, "x", lambda i, p: in_bx.at[i - 1, :, :, c])
            value = total(sum_ay[x, :, :, c], [in_bx[i, :, :, c] for i in range(nx - 1)])
        sum_b[:, :, :, c] = value.reshape(nz // 2, 2, rows_out, step).astype(jnp.bfloat16)
        send(
            base + 3,
            k,
            "near_z",
            lambda p: sum_b.at[:, p, :, c],
            lambda i: in_v.at[i - 1, :, :, c],
        )

    def return_near(k):
        c = columns[k]
        arrive(base + 3, k, "near_z", lambda i, p: in_v.at[i - 1, :, :, c])
        value = total(sum_b[:, zl, :, c], [in_v[0, :, :, c]])
        sum_w[:, :, c] = value.astype(jnp.bfloat16)
        send(more + 3, k, "far_z", lambda p: sum_w.at[p, :, c], lambda i: in_z.at[i - 1, :, c])

    def return_z(k):
        c = columns[k]
        arrive(more + 3, k, "far_z", lambda i, p: in_z.at[i - 1, :, c])
        value = total(sum_w[zh, :, c], [in_z[i, :, c] for i in range(nz // 2 - 1)])
        result_ref[:, c] = (hidden[:, c] + value).astype(jnp.bfloat16)

    wavefront(
        [
            (0, give),
            (FLIGHT, return_core),
            (2 * FLIGHT + 1, return_first),
            (3 * FLIGHT + 2, return_second),
            (4 * FLIGHT + 2, return_near),
            (5 * FLIGHT + 2, return_z),
        ]
    )
    for copy in sends:
        copy.wait_send()


def routed_layer(
    queries,
    cache,
    new_kv,
    q_gain,
    k_gain,
    out_weight,
    residual,
    norm_gain,
    expert_ids,
    combine_weight,
    prefix_len,
    w_gate_up,
    w_down,
):
    head_count = lax.axis_size("head")
    tok_count = lax.axis_size("tok")
    nz, ny, nx = DEPTH, head_count // DEPTH, tok_count // CORES
    width = out_weight.shape[1]
    rows_out, topk = expert_ids.shape
    experts_all = head_count * tok_count
    tokens = rows_out * experts_all
    capacity = max(2, 2 * rows_out * topk // experts_all)
    slots = experts_all * capacity
    hidden_units = w_down.shape[1]

    b16, f32 = jnp.bfloat16, jnp.float32
    vmem = pl.BlockSpec(memory_space=pltpu.VMEM)
    hbm = pl.BlockSpec(memory_space=pl.ANY)
    stages = 19 + 2 * nx
    query_rows = queries.shape[0]
    heads = queries.shape[1] // HD
    segment = cache.shape[1] + query_rows
    widest = max(nz, ny, nx, CORES) - 1
    scratch = [
        pltpu.VMEM(queries.shape, b16),
        pltpu.VMEM((tok_count, segment, 2 * HD), b16),
        pltpu.VMEM((heads * query_rows, HD), b16),
        pltpu.VMEM((heads * query_rows, HD), f32),
        pltpu.VMEM((heads * query_rows, 128), f32),
        pltpu.VMEM(queries.shape, b16),
        pltpu.VMEM((tok_count, nz // 2, 2, ny, rows_out, 256), b16),
        pltpu.VMEM((slots, tokens), b16),
        pltpu.VMEM((tokens, slots), b16),
        pltpu.VMEM(out_weight.shape, b16),
        pltpu.VMEM(w_gate_up.shape[1:], b16),
        pltpu.VMEM(w_down.shape[1:], b16),
        pltpu.VMEM((nz, ny, rows_out, width), b16),
        pltpu.VMEM((ny - 1, nz, rows_out, width), b16),
        pltpu.VMEM((nz // 2, 2, rows_out, width), b16),
        pltpu.VMEM((1, nz // 2, rows_out, width), b16),
        pltpu.VMEM((nz // 2, rows_out, width), b16),
        pltpu.VMEM((nz // 2 - 1, rows_out, width), b16),
        pltpu.VMEM((rows_out, width), f32),
        pltpu.VMEM((tok_count, nz // 2, 2, ny, rows_out, width + 128), b16),
        pltpu.VMEM((slots, 2 * hidden_units), f32),
        pltpu.VMEM((slots, hidden_units), b16),
        pltpu.VMEM((nx, CORES, nz, ny, rows_out, width), b16),
        pltpu.VMEM((nx, nz, ny, rows_out, width), b16),
        pltpu.VMEM((nx, nz, ny, rows_out, width), b16),
        pltpu.VMEM((nx - 1, nz, ny, rows_out, width), b16),
        pltpu.VMEM((ny - 1, nx, nz, rows_out, width), b16),
        pltpu.VMEM((nz, ny, rows_out, width), b16),
        pltpu.VMEM((nx, nz, rows_out, width), b16),
        pltpu.VMEM((nx - 1, nz, rows_out, width), b16),
        pltpu.VMEM((ny - 1, nz, rows_out, width), b16),
        pltpu.VMEM((nz // 2, 2, rows_out, width), b16),
        pltpu.VMEM((1, nz // 2, rows_out, width), b16),
        pltpu.VMEM((nz // 2, rows_out, width), b16),
        pltpu.VMEM((nz // 2 - 1, rows_out, width), b16),
        pltpu.SemaphoreType.DMA((3 + 3 * CHUNKS,)),
        pltpu.SemaphoreType.DMA((stages, CHUNKS, widest)),
        pltpu.SemaphoreType.DMA((stages, CHUNKS, widest)),
    ]
    return pl.pallas_call(
        functools.partial(layer_kernel, (nz, ny, nx, capacity)),
        out_shape=jax.ShapeDtypeStruct((rows_out, width), b16),
        in_specs=[hbm] * 3 + [vmem] * 3 + [hbm] + [vmem] * 4 + [hbm] * 2,
        out_specs=vmem,
        scratch_shapes=scratch,
        compiler_params=pltpu.CompilerParams(
            collective_id=0, has_side_effects=True, vmem_limit_bytes=VMEM_BYTES
        ),
    )(
        queries,
        cache,
        new_kv,
        q_gain.reshape(1, HD),
        k_gain.reshape(1, HD),
        prefix_len.reshape(1, 1),
        out_weight,
        residual,
        norm_gain.reshape(1, width),
        expert_ids.T,
        combine_weight.T,
        w_gate_up,
        w_down,
    )


def fits(tokens, width, experts, spans, heads):
    if spans > CORES * CHUNKS or heads % GROUP:
        return False
    return 12 * tokens * width <= VMEM_BYTES // 2 and experts <= 256


def per_device(
    queries,
    cache,
    new_kv,
    q_gain,
    k_gain,
    out_weight,
    residual,
    norm_gain,
    expert_ids,
    combine_weight,
    prefix_len,
    w_gate_up,
    w_down,
):
    head_count = lax.axis_size("head")
    tok_count = lax.axis_size("tok")
    query_rows = queries.shape[0]
    local_heads = queries.shape[1] // HD
    experts_all = head_count * tok_count
    tokens = query_rows * tok_count
    if fits(tokens, out_weight.shape[1], experts_all, tok_count, local_heads):
        return routed_layer(
            queries,
            cache,
            new_kv,
            q_gain,
            k_gain,
            out_weight,
            residual,
            norm_gain,
            expert_ids,
            combine_weight,
            prefix_len,
            w_gate_up,
            w_down,
        )
    cache_rows = cache.shape[1]
    segment = cache_rows + query_rows
    kv_index = lax.axis_index("head") * local_heads // (HEADS // KV_HEADS)
    query_normed = rms_scale(
        queries.reshape(query_rows, local_heads, HD).astype(jnp.float32), q_gain
    ).astype(jnp.bfloat16)
    own_block = jnp.concatenate(
        [
            lax.dynamic_index_in_dim(cache, kv_index, 0, keepdims=False),
            lax.dynamic_index_in_dim(new_kv, kv_index, 0, keepdims=False),
        ],
        axis=0,
    )
    key_part = rms_scale(own_block[:, :HD].astype(jnp.float32), k_gain).astype(jnp.bfloat16)
    key_block = jnp.concatenate([key_part, own_block[:, HD:]], axis=1)
    query_position = lax.axis_index("tok") * query_rows + jnp.arange(query_rows, dtype=jnp.int32)
    limit = prefix_len[0]
    piece = lax.all_gather(key_block, "tok", axis=0, tiled=True)
    position = jnp.arange(piece.shape[0], dtype=jnp.int32)
    shard = position // segment
    offset = position % segment
    in_cache = offset < cache_rows
    cache_position = shard * cache_rows + offset
    span_position = shard * query_rows + offset - cache_rows
    visible = jnp.where(
        in_cache[None, :],
        (cache_position < limit)[None, :],
        span_position[None, :] <= query_position[:, None],
    )
    scores = jnp.einsum(
        "qhd,kd->qhk", query_normed, piece[:, :HD], preferred_element_type=jnp.float32
    ) * HD ** (-0.5)
    weights = jnp.where(visible[:, None, :], jnp.exp(scores), 0.0)
    accum = jnp.einsum(
        "qhk,kd->qhd",
        weights.astype(jnp.bfloat16),
        piece[:, HD:],
        preferred_element_type=jnp.float32,
    )
    total = jnp.sum(weights, axis=2)
    accum, total = (accum, total)
    attn = (accum / total[:, :, None]).astype(jnp.bfloat16).reshape(query_rows, local_heads * HD)
    rows_out = query_rows // head_count
    full_proj = lax.psum(
        jnp.dot(attn, out_weight, preferred_element_type=jnp.float32).astype(jnp.bfloat16), "head"
    ).astype(jnp.float32)
    attn_proj = lax.dynamic_slice_in_dim(full_proj, lax.axis_index("head") * rows_out, rows_out, 0)
    hidden = residual.astype(jnp.float32) + attn_proj
    normed = rms_scale(hidden, norm_gain).astype(jnp.bfloat16)
    width = normed.shape[1]
    experts_all = head_count * tok_count
    topk = expert_ids.shape[1]
    capacity = max(2, 2 * rows_out * topk // experts_all)
    flat_ids = expert_ids.reshape(-1)
    onehot = (flat_ids[:, None] == jnp.arange(experts_all, dtype=jnp.int32)[None, :]).astype(
        jnp.int32
    )
    before = jnp.cumsum(onehot, axis=0) - onehot
    slot_index = jnp.sum(before * onehot, axis=1)
    target = (flat_ids * capacity + slot_index).reshape(rows_out, topk)
    matches = (
        target[:, :, None] == jnp.arange(experts_all * capacity, dtype=jnp.int32)[None, None, :]
    )
    placing = jnp.sum(matches.astype(jnp.int32), axis=1).astype(jnp.bfloat16)
    mixing = jnp.sum(
        jnp.where(matches, combine_weight.astype(jnp.float32)[:, :, None], 0.0), axis=1
    ).astype(jnp.bfloat16)
    outgoing = jnp.einsum("rs,rd->sd", placing, normed, preferred_element_type=jnp.float32).astype(
        jnp.bfloat16
    )
    outgoing = outgoing.reshape(experts_all, capacity, width)
    returned = lax.all_to_all(
        expert_block(
            lax.all_to_all(outgoing, ("head", "tok"), split_axis=0, concat_axis=0, tiled=True),
            w_gate_up[0],
            w_down[0],
        ),
        ("head", "tok"),
        split_axis=0,
        concat_axis=0,
        tiled=True,
    )
    back_rows = returned.reshape(experts_all * capacity, width)
    expert_sum = jnp.dot(mixing, back_rows, preferred_element_type=jnp.float32)
    return (hidden + expert_sum).astype(jnp.bfloat16)

def solution(mesh):
    placed = (
        P("tok", "head"),
        P(None, "tok", None),
        P(None, "tok", None),
        P(),
        P(),
        P("head", None),
        P(("tok", "head"), None),
        P(),
        P(("tok", "head"), None),
        P(("tok", "head"), None),
        P(),
        P(("head", "tok"), None, None),
        P(("head", "tok"), None, None),
    )
    return jax.shard_map(
        per_device, mesh=mesh, in_specs=placed, out_specs=P(("tok", "head"), None), check_vma=False
    )
```
